128 devices in a mesh: role: 4 (over x), grp: 32 (over z, y, core).
Axes of the slice: x: 4, y: 4, z: 4, core: 2. Of those that a mesh axis runs over, the one named last changes fastest.
Arguments:
- queries: bfloat16 [32, 16, 128, 576], P('grp', 'role'), may hold values from -400 to 400
- compressed_cache: bfloat16 [32, 16, 512, 576], P('grp', 'role'), may hold values from -7 to 7
- lengths: int32 [32, 16], P('grp', 'role'), may hold values from 16 to 512, as said below
- value_expand_matrix: bfloat16 [128, 512, 128], P(('role', 'grp')), may hold values from -0.25 to 0.25
- out_proj: bfloat16 [16384, 7168], P(('role', 'grp')), may hold values from -0.1875 to 0.1875
- residual: bfloat16 [32, 16, 7168], P('grp', 'role'), may hold values from -4 to 4
- norm_gain: bfloat16 [7168], replicated, may hold values from 0.25 to 1.75
- expert_ids: int32 [32, 16, 8], P('grp', 'role'), may hold values from 0 to 31, all different within a row; in each aligned block of 16 rows (0 to 15, 16 to 31, ..., all dimensions but the last counted through in order) at most 6 rows name the same one
- expert_gates: bfloat16 [32, 16, 8], P('grp', 'role'), may hold values from 0.099609375 to 0.59765625
- w_gate: bfloat16 [32, 7168, 2048], P('grp', None, 'role'), may hold values from -0.0625 to 0.0625
- w_up: bfloat16 [32, 7168, 2048], P('grp', None, 'role'), may hold values from -0.0625 to 0.0625
- w_down: bfloat16 [32, 2048, 7168], P('grp', 'role'), may hold values from -0.125 to 0.125
Outputs:
- layer_out: bfloat16 [32, 16, 7168], P('grp', 'role')
The draws below stay inside these ranges and needn't reach their ends.
Inputs may be any that keep to these rules, and one draw needn't show every extreme that they name: `expert_ids`: each token names 8 different experts. In every aligned block of 16 tokens (the tokens of one index of grp) no expert is named by more than 6 tokens; in some blocks one is named by exactly 6. `lengths`: some request has all 512 slots live.
All inputs are finite; a program needn't handle non-finite values.
Results may differ from the reference program's by a relative error of at most 0.015.
Values may be sent and summed in bfloat16 or wider, within the bound.
A program may use at most 128 MiB of HBM per device.

```python
import math
import jax
import jax.numpy as jnp
import numpy as np
from jax import lax

H = 128
KVL = 512
VD = 128
D = 7168
FF = 2048
TOPK = 8
CTX = 512
KV_ALL = 576
GRP_TOK = 16
GROUPS = 32
TOKENS = 512
EXPERTS = 32
CAP = 6


def cache_parts(key):
    base = jax.random.truncated_normal(jax.random.fold_in(key, 101), -6.0, 6.0, (GROUPS, GRP_TOK, CTX, KV_ALL), jnp.float32)
    return base


def draw_compressed_cache(key, part):
    base = cache_parts(key)
    return base.astype(jnp.bfloat16)


def draw_queries(key, part):
    key = jax.random.fold_in(key, 2)
    result = jax.random.truncated_normal(key, -6.0, 6.0, (GROUPS, GRP_TOK, H, KV_ALL), jnp.float32)
    return result.astype(jnp.bfloat16)


def draw_lengths(key, part):
    key = jax.random.fold_in(key, 3)
    leading_key, second_key, third_key = jax.random.split(key, 3)
    first_draw = jax.random.randint(leading_key, (GROUPS * GRP_TOK,), 0, CTX - 15)
    second_draw = jax.random.randint(second_key, (GROUPS * GRP_TOK,), 0, CTX - 15)
    spread_len = 16 + jnp.minimum(first_draw, second_draw)
    full_spot = jax.random.randint(third_key, (), 0, GROUPS * GRP_TOK)
    spread_len = jnp.where(jnp.arange(GROUPS * GRP_TOK) == full_spot, CTX, spread_len)
    return spread_len.reshape(GROUPS, GRP_TOK).astype(jnp.int32)


def with_spikes(entries, key, source, target, blocks, factor):
    owner, partner = [(jnp.arange(entries.shape[dim]) // (entries.shape[dim] // blocks)).reshape([-1 if axis == dim else 1 for axis in range(entries.ndim)]) for dim in (source, target)]
    chosen = jax.random.permutation(key, blocks)[partner]
    strong = (owner == chosen) | (owner == (partner + blocks // 2) % blocks)
    return jnp.where(strong, factor * entries, entries)


def level_of(key, shape, cuts, smallest, top_value):
    level, own = 1.0, jax.random.fold_in(key, 6)
    for axis_at, blocks in cuts:
        steps = jnp.exp(jax.random.uniform(jax.random.fold_in(own, axis_at), (blocks,), jnp.float32, smallest / len(cuts), top_value / len(cuts)))
        level = level * jnp.repeat(steps, shape[axis_at] // blocks).reshape([-1 if axis == axis_at else 1 for axis in range(len(shape))])
    return level


def deal_out(key, own, number, rows, number_of, top, bound, slope):
    sequence = jax.random.permutation(key, number_of)
    heavy_load, common = load_shares(number_of, rows * top, bound, slope, True), load_shares(number_of, rows * top, bound, slope, False)
    places = jnp.arange(number_of)

    def named(tallies, offset_by):
        used = int((tallies > 0).sum())
        fixed = max(1, used // 4)
        moved = fixed + (places - fixed + offset_by * (used - fixed)) % max(1, number_of - fixed)
        return jnp.zeros((number_of,), jnp.int32).at[sequence[jnp.where(places < fixed, places, moved)]].set(jnp.asarray(tallies, jnp.int32))

    tallies = jnp.where(number % 4 == 0, named(heavy_load, number // 4), named(common, number - number // 4 - 1))
    mixed = jax.random.permutation(jax.random.fold_in(own, 3), number_of)
    donor, taker = mixed[0:number_of // 2 * 2:2], mixed[1:number_of // 2 * 2:2]
    margin = jnp.minimum(tallies[donor] - 1, bound - tallies[taker]) // 2
    margin = jnp.where((donor == sequence[0]) | (taker == sequence[0]) | (tallies[taker] == 0), 0, jnp.maximum(margin, 0))
    moved = jax.random.randint(jax.random.fold_in(own, 4), (number_of // 2,), 0, 1 << 20) % (margin + 1)
    tallies = tallies.at[donor].add(-moved).at[taker].add(moved)
    members = jnp.searchsorted(jnp.cumsum(tallies), jnp.arange(rows * top), side="right").astype(jnp.int32)
    table = members.reshape(top, rows).T
    table = table[jax.random.permutation(jax.random.fold_in(own, 1), rows)]
    offset_by = jax.random.randint(jax.random.fold_in(own, 2), (rows, 1), 0, top)
    return jnp.take_along_axis(table, (jnp.arange(top)[None, :] + offset_by) % top, axis=1)


def load_shares(count, total, bound, slope, full):
    weights = [(1 << 20) // math.isqrt(grade ** slope) + 1 for grade in range(1, count + 1)]
    largest = bound if full else min(bound, max(-(-total // count), total * weights[0] // sum(weights)))
    least = 1 if total - largest >= count - 1 else 0
    holding, surplus = [largest] + [least] * (count - 1), total - largest - least * (count - 1)
    while surplus > 0:
        candidates = [i for i in range(1, count) if holding[i] < largest] or [i for i in range(1, count) if holding[i] < bound]
        pool, budget = sum([weights[i] for i in candidates]), surplus
        for i in candidates:
            extra = min(bound - holding[i], max(1, budget * weights[i] // pool), surplus)
            holding[i] = holding[i] + extra
            surplus = surplus - extra
    return np.array(holding)


def noise(own_key, shape, width, bound, shards=(), kind=jnp.bfloat16):
    factor_of = level_of(own_key, shape, shards, -0.22, 0.18) if shards else 1.0
    values = jax.random.normal(own_key, shape, jnp.float32) * width * factor_of
    return jnp.minimum(jnp.maximum(values, -bound), bound).astype(kind)


def gaussian_with(rng, dims, scale, limit, cuts, heavy, held_as=jnp.bfloat16):
    values = scale * jax.random.normal(rng, dims, jnp.float32)
    if cuts:
        values = values * level_of(rng, dims, cuts, -0.22, 0.18)
    return jnp.clip(with_spikes(values, jax.random.fold_in(rng, 3), *heavy), -limit, limit).astype(held_as)


def setup_inputs(seed: int = 0) -> dict:
    streams_of = jax.random.split(jax.random.key(seed), 13)
    queries = draw_queries(jax.random.fold_in(streams_of[12], 71), 0)
    compressed_cache = draw_compressed_cache(jax.random.fold_in(streams_of[12], 71), 0)
    lengths = draw_lengths(jax.random.fold_in(streams_of[12], 71), 0)
    value_expand_matrix = noise(streams_of[3], (H, KVL, VD), KVL ** -0.5, 0.25, ((0, 128),))
    out_proj = gaussian_with(streams_of[4], (H * VD, D), (H * VD) ** -0.5, 0.1875, ((0, 128),), (0, 1, 128, 5.5))
    residual = noise(streams_of[5], (GROUPS, GRP_TOK, D), 0.5, 4.0, ((0, 32), (1, 4)))
    norm_gain = jnp.clip(1.0 + 0.15 * jax.random.normal(streams_of[6], (D,), jnp.float32), 0.25, 1.75).astype(jnp.bfloat16)
    expert_ids_keys = jax.random.split(jax.random.fold_in(streams_of[7], 1), GROUPS * GRP_TOK // GRP_TOK)
    expert_ids_turns = jax.random.permutation(jax.random.fold_in(streams_of[7], 3), GROUPS * GRP_TOK // GRP_TOK)
    expert_ids = jax.vmap(lambda own, number: deal_out(jax.random.fold_in(streams_of[7], 2), own, number, GRP_TOK, EXPERTS, TOPK, CAP, 2))(expert_ids_keys, expert_ids_turns).reshape((GROUPS, GRP_TOK, TOPK))
    expert_gates = jnp.clip(0.099609375 + 0.49804688 * jax.random.uniform(streams_of[8], (GROUPS, GRP_TOK, TOPK), jnp.float32) ** level_of(streams_of[8], (GROUPS, GRP_TOK, TOPK), ((0, 32), (1, 4)), -0.2, 0.2), 0.099609375, 0.59765625).astype(jnp.bfloat16)
    w_gate = noise(streams_of[9], (EXPERTS, D, FF), D ** -0.5, 0.0625, ((0, 32), (2, 4)))
    w_up = noise(streams_of[10], (EXPERTS, D, FF), D ** -0.5, 0.0625, ((0, 32), (2, 4)))
    w_down = noise(streams_of[11], (EXPERTS, FF, D), FF ** -0.5, 0.125, ((0, 32), (1, 4)))
    return dict(queries=queries, compressed_cache=compressed_cache, lengths=lengths, value_expand_matrix=value_expand_matrix, out_proj=out_proj, residual=residual, norm_gain=norm_gain, expert_ids=expert_ids, expert_gates=expert_gates, w_gate=w_gate, w_up=w_up, w_down=w_down)


score_scale = 192.0 ** (-0.5)
norm_eps = 1e-06

def attend(inputs):
    query, cache, length = inputs
    scores = jnp.dot(query, cache.T, preferred_element_type=jnp.float32) * score_scale
    live_keys = jnp.arange(CTX, dtype=jnp.int32)[None, :] < length
    row_max = lax.optimization_barrier(jnp.max(jnp.where(live_keys, scores, -1e+30), axis=-1, keepdims=True))
    exp_terms = jnp.exp(jnp.where(live_keys, scores - row_max, -1e+30))
    exp_total = lax.optimization_barrier(jnp.sum(exp_terms, axis=-1, keepdims=True))
    weighted_sum = jnp.dot(exp_terms.astype(jnp.bfloat16), cache[:, :KVL], preferred_element_type=jnp.float32) / exp_total
    return weighted_sum.astype(jnp.bfloat16)

def reference(queries, compressed_cache, lengths, value_expand_matrix, out_proj, residual, norm_gain, expert_ids, expert_gates, w_gate, w_up, w_down):
    query_rows = queries.reshape(TOKENS, H, KV_ALL)
    cache_rows = compressed_cache.reshape(TOKENS, CTX, KV_ALL)
    length_rows = lengths.reshape(TOKENS).astype(jnp.int32)
    latent_result = lax.map(attend, (query_rows, cache_rows, length_rows))
    value_rows = jnp.einsum('gri,rix->grx', latent_result.astype(jnp.float32), value_expand_matrix.astype(jnp.float32)).astype(jnp.bfloat16)
    attention = jnp.dot(value_rows.reshape(TOKENS, H * VD), out_proj, preferred_element_type=jnp.float32)
    stream = residual.reshape(TOKENS, D).astype(jnp.float32) + attention
    scale_rows = lax.rsqrt(lax.optimization_barrier(jnp.mean(stream * stream, axis=-1, keepdims=True)) + norm_eps)
    normed = (stream * scale_rows * norm_gain.astype(jnp.float32)).astype(jnp.bfloat16)
    route_ids = expert_ids.reshape(TOKENS, TOPK).astype(jnp.int32)
    gate_values = expert_gates.reshape(TOKENS, TOPK).astype(jnp.float32)
    picked = route_ids[:, :, None] == jnp.arange(EXPERTS, dtype=jnp.int32)[None, None, :]
    gate_table = lax.optimization_barrier(jnp.sum(jnp.where(picked, gate_values[:, :, None], jnp.zeros((), jnp.float32)), axis=1))
    routed = jnp.any(picked, axis=1)
    row_limit = GROUPS * CAP

    def one_expert(carry_sum, inputs):
        weight_gate, weight_up, weight_down, gate_column, chosen = inputs
        row_order = jnp.argsort(jnp.where(chosen, 0, 1).astype(jnp.int32), stable=True)[:row_limit].astype(jnp.int32)
        picked_rows = normed[row_order]
        gate_proj = jnp.dot(picked_rows, weight_gate, preferred_element_type=jnp.float32)
        up_proj = jnp.dot(picked_rows, weight_up, preferred_element_type=jnp.float32)
        activated = (jax.nn.silu(gate_proj) * up_proj).astype(jnp.bfloat16)
        down_proj = jnp.dot(activated, weight_down, preferred_element_type=jnp.float32)
        carry_sum = carry_sum.at[row_order].add(gate_column[row_order][:, None] * down_proj)
        return (carry_sum, None)
    expert_sum, _ = lax.scan(one_expert, jnp.zeros((TOKENS, D), jnp.float32), (w_gate, w_up, w_down, gate_table.T, routed.T))
    return (stream + expert_sum).astype(jnp.bfloat16).reshape(GROUPS, GRP_TOK, D)
```

```python
import jax
import jax.numpy as jnp
from jax import lax
from jax.experimental import pallas as pl
from jax.experimental.pallas import tpu as pltpu
from jax.sharding import PartitionSpec as P

MESH = pl.DeviceIdType.MESH
F32 = jnp.float32
BF16 = jnp.bfloat16

score_scale = 192.0 ** (-0.5)
norm_eps = 1e-06

D = 7168
QUARTER = 1792
PARTS = (
    (0, 640, (0, 1, 2)),
    (640, 640, (1, 2, 0)),
    (1280, 512, (2, 0, 1)),
)
WIDE = 640


def coordinates():
    grp = lax.axis_index("grp")
    return lax.axis_index("role"), grp // 8, (grp // 2) % 4, grp % 2


def device(x, z, y, c):
    return {"role": x, "grp": z * 8 + y * 2 + c}


def dot(a, b):
    return jnp.dot(a, b, preferred_element_type=F32)


def onehot(shape, source_of_row):
    rows = lax.broadcasted_iota(jnp.int32, shape, 0)
    columns = lax.broadcasted_iota(jnp.int32, shape, 1)
    return (columns == source_of_row(rows)).astype(BF16)


def kernel(
    len_ref,
    res_ref,
    gain_ref,
    ids_ref,
    gates_ref,
    q_hbm,
    cache_hbm,
    ve_hbm,
    op_hbm,
    wg_hbm,
    wu_hbm,
    wd_hbm,
    out_ref,
    q_buf,
    cache_buf,
    op_buf,
    wg_buf,
    wu_buf,
    wd_buf,
    ve_buf,
    a2a_send,
    a2a_recv,
    val_f32,
    val_send,
    val_recv,
    p_a,
    p_b,
    p_c,
    r1_a,
    r1_b,
    r1_c,
    s1_a,
    s1_b,
    s1_c,
    r2_a,
    r2_b,
    r2_c,
    s2_a,
    s2_b,
    s2_c,
    r3_a,
    r3_b,
    r3_c,
    n_a,
    n_b,
    n_c,
    stream_buf,
    acc_g,
    acc_u,
    act_buf,
    far_a,
    far_b,
    far_c,
    last_send,
    load_sem,
    ve_send_sem,
    ve_recv_sem,
    op_send_sem,
    op_recv_sem,
    a2a_send_sem,
    a2a_recv_sem,
    val_send_sem,
    val_recv_sem,
    rs_send_sem,
    rs_recv_sem,
    ag_send_sem,
    ag_recv_sem,
    pair_send_sem,
    pair_recv_sem,
    far_send_sem,
    far_recv_sem,
    last_send_sem,
    last_recv_sem,
):
    x, z, y, c = coordinates()
    zy = z * 4 + y
    other = 1 - c
    here = (x, z, y)
    me = device(x, z, y, c)
    sibling = device(x, z, y, other)
    sends = []

    def peer(axis, step):
        at = [x, z, y]
        at[axis] = (at[axis] + step) % 4
        return device(at[0], at[1], at[2], c)

    def remote(src, dst, send_sem, recv_sem, to):
        return pltpu.make_async_remote_copy(
            src_ref=src,
            dst_ref=dst,
            send_sem=send_sem,
            recv_sem=recv_sem,
            device_id=to,
            device_id_type=MESH,
        )

    def send(src, dst, send_sem, recv_sem, to):
        copy = remote(src, dst, send_sem, recv_sem, to)
        copy.start()
        sends.append(copy)

    def arrived(dst, send_sem, recv_sem):
        remote(dst, dst, send_sem, recv_sem, me).wait_recv()

    def zy_peer(step):
        p = (zy + step) % 16
        return p, device(x, p // 4, p % 4, c)

    barrier = pltpu.get_barrier_semaphore()

    def greet(step, carry):
        _, to = zy_peer(step)
        pl.semaphore_signal(barrier, inc=1, device_id=to, device_id_type=MESH)
        return carry

    lax.fori_loop(1, 16, greet, 0)
    for step in range(1, 4):
        for core in (c, other):
            pl.semaphore_signal(
                barrier, inc=1, device_id=device((x + step) % 4, z, y, core), device_id_type=MESH
            )
    pl.semaphore_signal(barrier, inc=1, device_id=sibling, device_id_type=MESH)

    load_q = pltpu.make_async_copy(q_hbm.at[0], q_buf, load_sem.at[0])
    load_cache = pltpu.make_async_copy(cache_hbm.at[0], cache_buf, load_sem.at[1])
    ve_own = ve_buf.at[x, :, pl.ds(pl.multiple_of(c * 128, 128), 128)]
    load_ve = pltpu.make_async_copy(ve_hbm.at[0], ve_own, load_sem.at[2])
    op_own = op_buf.at[pl.ds(pl.multiple_of(c * 128, 128), 128), :]
    load_op = pltpu.make_async_copy(op_hbm, op_own, load_sem.at[3])
    load_wg = pltpu.make_async_copy(wg_hbm.at[0], wg_buf, load_sem.at[4])
    load_wu = pltpu.make_async_copy(wu_hbm.at[0], wu_buf, load_sem.at[5])
    load_wd = pltpu.make_async_copy(wd_hbm.at[0], wd_buf, load_sem.at[6])
    for load in (load_q, load_cache, load_ve, load_op, load_wg, load_wu, load_wd):
        load.start()
    load_q.wait()
    load_cache.wait()

    order = onehot(
        (128, 128), lambda i: (i % 8) // 2 * 32 + (i // 8) * 2 + i % 2
    )

    def attend(t):
        query = q_buf[t]
        cache = cache_buf[t]
        scores = (
            lax.dot_general(query, cache, (((1,), (1,)), ((), ())), preferred_element_type=F32)
            * score_scale
        )
        live = lax.broadcasted_iota(jnp.int32, scores.shape, 1) < len_ref[0, t]
        top = jnp.max(jnp.where(live, scores, -1e30), axis=-1, keepdims=True)
        terms = jnp.exp(jnp.where(live, scores - top, -1e30))
        total = jnp.sum(terms, axis=-1, keepdims=True)
        latent = (dot(terms.astype(BF16), cache[:, :512]) / total).astype(BF16)
        return dot(order, latent).reshape(16, 8, 512)

    for pair in range(2):
        both = jnp.concatenate([attend(2 * pair), attend(2 * pair + 1)], axis=1)
        a2a_send[:, pair * 16 : pair * 16 + 16, :] = both.astype(BF16)

    pl.semaphore_wait(barrier, 22)

    def a2a_start(step, carry):
        p, to = zy_peer(step)
        remote(
            a2a_send.at[p], a2a_recv.at[zy], a2a_send_sem.at[step], a2a_recv_sem.at[step], to
        ).start()
        return carry

    lax.fori_loop(1, 16, a2a_start, 0)

    load_ve.wait()
    for step in range(1, 4):
        for k, core in enumerate((c, other)):
            send(
                ve_own,
                ve_own,
                ve_send_sem.at[2 * step + k],
                ve_recv_sem.at[2 * step + k],
                device((x + step) % 4, z, y, core),
            )
    send(ve_own, ve_own, ve_send_sem.at[0], ve_recv_sem.at[0], sibling)
    load_op.wait()
    send(op_own, op_own, op_send_sem.at[0], op_recv_sem.at[0], sibling)

    a2a_recv[zy] = a2a_send[zy]

    def a2a_wait(step, carry):
        _, to = zy_peer(step)
        p, _ = zy_peer(16 - step)
        copy = remote(
            a2a_send.at[zy], a2a_recv.at[p], a2a_send_sem.at[step], a2a_recv_sem.at[step], to
        )
        copy.wait_send()
        copy.wait_recv()
        return carry

    lax.fori_loop(1, 16, a2a_wait, 0)
    for step in range(1, 4):
        for k, core in enumerate((c, other)):
            arrived(
                ve_buf.at[(x + 4 - step) % 4, :, pl.ds(pl.multiple_of(core * 128, 128), 128)],
                ve_send_sem.at[2 * step + k],
                ve_recv_sem.at[2 * step + k],
            )
    arrived(
        ve_buf.at[x, :, pl.ds(pl.multiple_of(other * 128, 128), 128)],
        ve_send_sem.at[0],
        ve_recv_sem.at[0],
    )

    latents = a2a_recv[...].reshape(512, 512)
    head_of_row = lax.broadcasted_iota(jnp.int32, (512, 128), 0) % 8
    values = jnp.zeros((512, 128), F32)
    for h in range(4):
        product = dot(latents, ve_buf[h])
        values = jnp.where(head_of_row == 2 * h, product[:, :128], values)
        values = jnp.where(head_of_row == 2 * h + 1, product[:, 128:], values)
    val_f32[...] = values
    for h in range(4):
        val_send[h] = jnp.concatenate(
            [val_f32[pl.ds(2 * h, 64, stride=8), :], val_f32[pl.ds(2 * h + 1, 64, stride=8), :]],
            axis=1,
        ).astype(BF16)
    for step in range(1, 4):
        to = (x + step) % 4
        send(
            val_send.at[to],
            val_recv.at[x],
            val_send_sem.at[step],
            val_recv_sem.at[step],
            device(to, z, y, c),
        )
    val_recv[x] = val_send[x]
    arrived(
        op_buf.at[pl.ds(pl.multiple_of(other * 128, 128), 128), :],
        op_send_sem.at[0],
        op_recv_sem.at[0],
    )
    for step in range(1, 4):
        arrived(val_recv.at[(x + 4 - step) % 4], val_send_sem.at[step], val_recv_sem.at[step])

    token_order = onehot((256, 256), lambda i: (i % 16) // 4 * 64 + (i // 16) * 4 + i % 4)
    rows = dot(token_order, val_recv[...].reshape(256, 256)).astype(BF16)

    own_rows = onehot((16, 8), lambda i: jnp.where(i // 4 == x, i % 4, -1))

    p_refs = (p_a, p_b, p_c)
    r_refs = ((r1_a, r2_a, r3_a), (r1_b, r2_b, r3_b), (r1_c, r2_c, r3_c))
    s_refs = ((s1_a, s2_a), (s1_b, s2_b), (s1_c, s2_c))
    n_refs = (n_a, n_b, n_c)

    def slot(round_, part, phase, step):
        return ((round_ * 3 + part) * 3 + phase) * 4 + step

    def left_axes(part, phase):
        done = PARTS[part][2][:phase]
        return [a for a in (0, 1, 2) if a not in done]

    def rs_source(part, phase):
        return p_refs[part] if phase == 0 else s_refs[part][phase - 1]

    def block(part, phase, index):
        axis = PARTS[part][2][phase]
        return tuple(index if a == axis else slice(None) for a in left_axes(part, phase))

    def rs_send(round_, part, phase):
        axis = PARTS[part][2][phase]
        for step in range(1, 4):
            s = slot(round_, part, phase, step)
            send(
                rs_source(part, phase).at[block(part, phase, (here[axis] + step) % 4)],
                r_refs[part][phase].at[step - 1],
                rs_send_sem.at[s],
                rs_recv_sem.at[s],
                peer(axis, step),
            )

    def rs_wait(round_, part, phase):
        for step in range(1, 4):
            s = slot(round_, part, phase, step)
            arrived(r_refs[part][phase].at[step - 1], rs_send_sem.at[s], rs_recv_sem.at[s])

    def rs_sum(part, phase):
        axis = PARTS[part][2][phase]
        source = rs_source(part, phase).at[block(part, phase, here[axis])]
        received = r_refs[part][phase]

        def total(*at):
            value = source[at].astype(F32)
            for k in range(3):
                value = value + received[(k, *at)].astype(F32)
            return value

        if phase == 2:
            return total()
        target = s_refs[part][phase]

        def add(i, carry):
            if phase == 1:
                target[i] = total(i).astype(BF16)
            else:
                for j in range(4):
                    target[i, j] = total(i, j).astype(BF16)
            return carry

        lax.fori_loop(0, 4, add, 0)
        return None

    def reduce_rows(round_, finish):
        for phase in range(3):
            for part in range(3):
                rs_wait(round_, part, phase)
                result = rs_sum(part, phase)
                if phase < 2:
                    rs_send(round_, part, phase + 1)
                else:
                    finish(part, result)

    residual = res_ref[...]
    for part, (offset, width, _) in enumerate(PARTS):

        def project(k, carry, part=part, offset=offset, width=width):
            columns = pl.ds(pl.multiple_of(k * QUARTER + offset, 128), width)
            p_refs[part][k] = dot(rows, op_buf[:, columns]).astype(BF16).reshape(4, 4, 16, width)
            own = p_refs[part].at[k, z, y]
            own[...] = (own[...].astype(F32) + dot(own_rows, res_ref[:, columns])).astype(BF16)
            return carry

        lax.fori_loop(0, 4, project, 0)
        rs_send(0, part, 0)

    lane = lax.broadcasted_iota(jnp.int32, (8, 128), 1)
    table = jnp.zeros((8, 128), F32)
    for k in range(8):
        table = table + jnp.where(ids_ref[:, k : k + 1] == lane, gates_ref[:, k : k + 1], 0.0)
    table = dot(own_rows, table.astype(BF16))

    squares = []

    def keep_stream(part, result):
        offset, width, _ = PARTS[part]
        stream_buf[:, offset : offset + width] = result
        squares.append(jnp.sum(result * result, axis=-1, keepdims=True))
        columns = pl.ds(pl.multiple_of(x * QUARTER + offset, 128), width)
        n_refs[part][c, x, z, y, :, :width] = (result * gain_ref[:, columns].astype(F32)).astype(
            BF16
        )

    reduce_rows(0, keep_stream)
    square = squares[0] + squares[1] + squares[2]
    high = square.astype(BF16).astype(F32)
    lane16 = lax.broadcasted_iota(jnp.int32, (16, 128), 1)
    extra = jnp.where(lane16 == 32, high, jnp.where(lane16 == 33, square - high, table))
    n_c[c, x, z, y, :, 512:] = extra.astype(BF16)

    def ag_block(part, phase, index):
        axes = PARTS[part][2]
        at = [slice(None)] * 3
        for a in axes[:phase]:
            at[a] = here[a]
        at[axes[phase]] = index
        return n_refs[part].at[(c, *at)]

    for phase in (2, 1, 0):
        for part in range(3):
            axis = PARTS[part][2][phase]
            if phase < 2:
                before = PARTS[part][2][phase + 1]
                for step in range(1, 4):
                    s = slot(0, part, phase + 1, step)
                    arrived(
                        ag_block(part, phase + 1, (here[before] + 4 - step) % 4),
                        ag_send_sem.at[s],
                        ag_recv_sem.at[s],
                    )
            for step in range(1, 4):
                s = slot(0, part, phase, step)
                own = ag_block(part, phase, here[axis])
                send(own, own, ag_send_sem.at[s], ag_recv_sem.at[s], peer(axis, step))
    for part in range(3):
        axis = PARTS[part][2][0]
        for step in range(1, 4):
            s = slot(0, part, 0, step)
            arrived(
                ag_block(part, 0, (here[axis] + 4 - step) % 4),
                ag_send_sem.at[s],
                ag_recv_sem.at[s],
            )
        half = n_refs[part].at[c]
        send(half, half, pair_send_sem.at[part], pair_recv_sem.at[part], sibling)

    load_wg.wait()
    load_wu.wait()
    load_wd.wait()
    expert = z * 8 + y * 2 + c
    lanes = lax.broadcasted_iota(jnp.int32, (256, 128), 1)
    for half, core in enumerate((c, other)):
        if half == 1:
            for part in range(3):
                arrived(n_refs[part].at[core], pair_send_sem.at[part], pair_recv_sem.at[part])
        acc_g[...] = jnp.zeros_like(acc_g)
        acc_u[...] = jnp.zeros_like(acc_u)
        for part, (offset, width, _) in enumerate(PARTS):

            def up(k, carry, part=part, offset=offset, width=width, core=core):
                chunk = n_refs[part][core, k, :, :, :, :width].reshape(256, width)
                depth = pl.ds(pl.multiple_of(k * QUARTER + offset, 128), width)
                acc_g[...] += dot(chunk, wg_buf[depth, :])
                acc_u[...] += dot(chunk, wu_buf[depth, :])
                return carry

            lax.fori_loop(0, 4, up, 0)
        extra = jnp.zeros((256, 128), F32)
        for k in range(4):
            extra = extra + n_c[core, k, :, :, :, 512:].reshape(256, 128).astype(F32)
        weight = jnp.sum(jnp.where(lanes == expert, extra, 0.0), axis=-1, keepdims=True)
        square = jnp.sum(
            jnp.where((lanes == 32) | (lanes == 33), extra, 0.0), axis=-1, keepdims=True
        )
        scale = lax.rsqrt(square * (1.0 / D) + norm_eps)
        gate = acc_g[...] * scale
        act = gate / (1.0 + jnp.exp(-gate)) * (acc_u[...] * scale)
        act_buf[half] = (act * weight).astype(BF16)

    for copy in sends:
        copy.wait_send()
    sends.clear()

    far_refs = (far_a, far_b, far_c)
    for part, (offset, width, _) in enumerate(PARTS):

        def down_far(k, carry, part=part, offset=offset, width=width):
            columns = pl.ds(pl.multiple_of(k * QUARTER + offset, 128), width)
            n_refs[part][c, k, :, :, :, :width] = (
                dot(act_buf[1], wd_buf[:, columns]).astype(BF16).reshape(4, 4, 16, width)
            )
            return carry

        lax.fori_loop(0, 4, down_far, 0)
        send(
            n_refs[part].at[c, :, :, :, :, pl.ds(0, width)],
            far_refs[part],
            far_send_sem.at[part],
            far_recv_sem.at[part],
            sibling,
        )
    for part, (offset, width, _) in enumerate(PARTS):
        arrived(far_refs[part], far_send_sem.at[part], far_recv_sem.at[part])

        def down(k, carry, part=part, offset=offset, width=width):
            columns = pl.ds(pl.multiple_of(k * QUARTER + offset, 128), width)
            total = dot(act_buf[0], wd_buf[:, columns])
            total = total + far_refs[part][k].reshape(256, width).astype(F32)
            p_refs[part][k] = total.astype(BF16).reshape(4, 4, 16, width)
            return carry

        lax.fori_loop(0, 4, down, 0)
        rs_send(1, part, 0)

    def add_stream(part, result):
        offset, width, _ = PARTS[part]
        stream_buf[:, offset : offset + width] += result

    reduce_rows(1, add_stream)

    rounded = stream_buf[...].astype(BF16)
    last = jnp.zeros((64, 512), F32)
    for j in range(4):
        pick = onehot(
            (64, 16), lambda i: jnp.where((i % 16) // 4 == j, i // 16 * 4 + i % 4, -1)
        )
        piece = rounded[:, j * 512 : min(j * 512 + 512, QUARTER)]
        moved = dot(pick, piece)
        if moved.shape[1] < 512:
            moved = jnp.concatenate([moved, jnp.zeros((64, 512 - moved.shape[1]), F32)], axis=1)
        last = last + moved
    last_send[...] = last.astype(BF16).reshape(4, 16, 512)
    for step in range(1, 4):
        to = (x + step) % 4
        send(
            last_send.at[to],
            out_ref.at[x],
            last_send_sem.at[step],
            last_recv_sem.at[step],
            device(to, z, y, c),
        )
    out_ref[x] = last_send[x]
    for step in range(1, 4):
        arrived(out_ref.at[(x + 4 - step) % 4], last_send_sem.at[step], last_recv_sem.at[step])
    for copy in sends:
        copy.wait_send()


def per_device(
    queries,
    compressed_cache,
    lengths,
    value_expand_matrix,
    out_proj,
    residual,
    norm_gain,
    expert_ids,
    expert_gates,
    w_gate,
    w_up,
    w_down,
):
    vmem = lambda *shape, dtype=BF16: pltpu.VMEM(shape, dtype)
    widths = [w for _, w, _ in PARTS]
    dma = lambda n: pltpu.SemaphoreType.DMA((n,))
    scratch = [
        vmem(4, 128, 576),
        vmem(4, 512, 576),
        vmem(256, D),
        vmem(D, 512),
        vmem(D, 512),
        vmem(512, D),
        vmem(4, 512, 256),
        vmem(16, 32, 512),
        vmem(16, 32, 512),
        vmem(512, 128, dtype=F32),
        vmem(4, 64, 256),
        vmem(4, 64, 256),
        *[vmem(4, 4, 4, 16, w) for w in widths],
        *[vmem(3, 4, 4, 16, w) for w in widths],
        *[vmem(4, 4, 16, w) for w in widths],
        *[vmem(3, 4, 16, w) for w in widths],
        *[vmem(4, 16, w) for w in widths],
        *[vmem(3, 16, w) for w in widths],
        *[vmem(2, 4, 4, 4, 16, WIDE) for w in widths],
        vmem(16, QUARTER, dtype=F32),
        vmem(256, 512, dtype=F32),
        vmem(256, 512, dtype=F32),
        vmem(2, 256, 512),
        *[vmem(4, 4, 4, 16, w) for w in widths],
        vmem(4, 16, 512),
        dma(7),
        dma(8),
        dma(8),
        dma(1),
        dma(1),
        dma(16),
        dma(16),
        dma(4),
        dma(4),
        dma(72),
        dma(72),
        dma(36),
        dma(36),
        dma(3),
        dma(3),
        dma(3),
        dma(3),
        dma(4),
        dma(4),
    ]
    in_vmem = pl.BlockSpec(memory_space=pltpu.VMEM)
    anywhere = pl.BlockSpec(memory_space=pl.ANY)
    pad = lambda a: jnp.concatenate([a, jnp.zeros_like(a)], axis=0)
    result = pl.pallas_call(
        kernel,
        out_shape=jax.ShapeDtypeStruct((4, 16, 512), BF16),
        in_specs=[pl.BlockSpec(memory_space=pltpu.SMEM)] + [in_vmem] * 4 + [anywhere] * 7,
        out_specs=in_vmem,
        scratch_shapes=scratch,
        compiler_params=pltpu.CompilerParams(
            collective_id=0, has_side_effects=True, vmem_limit_bytes=64 << 20
        ),
        cost_estimate=pl.CostEstimate(
            flops=14 * 10**9, bytes_accessed=28 * 10**6, transcendentals=600_000
        ),
        name="layer",
    )(
        lengths,
        pad(residual[0]),
        norm_gain[None],
        pad(expert_ids[0]),
        pad(expert_gates[0].astype(F32)),
        queries,
        compressed_cache,
        value_expand_matrix,
        out_proj,
        w_gate,
        w_up,
        w_down,
    )
    result = result.reshape(4, 4, 4, 512).transpose(2, 0, 1, 3).reshape(4, 4, 2048)
    return result[:, :, :QUARTER].reshape(1, 4, D)


def solution(mesh):
    in_specs = (
        P("grp", "role", None, None),
        P("grp", "role", None, None),
        P("grp", "role"),
        P(("role", "grp"), None, None),
        P(("role", "grp"), None),
        P("grp", "role", None),
        P(),
        P("grp", "role", None),
        P("grp", "role", None),
        P("grp", None, "role"),
        P("grp", None, "role"),
        P("grp", "role", None),
    )
    out_specs = P("grp", "role", None)
    return jax.shard_map(
        per_device, mesh=mesh, in_specs=in_specs, out_specs=out_specs, check_vma=False
    )
```

```python
import jax
import jax.numpy as jnp
from jax import lax
from jax.experimental import pallas as pl
from jax.experimental.pallas import tpu as pltpu
from jax.sharding import PartitionSpec as P

MESH = pl.DeviceIdType.MESH
F32 = jnp.float32
BF16 = jnp.bfloat16

score_scale = 192.0 ** (-0.5)
norm_eps = 1e-06

D = 7168
QUARTER = 1792
FLOWS = (
    (0, 384, (0, 1, 2)),
    (384, 256, (1, 2, 0)),
    (640, 256, (2, 0, 1)),
    (896, 256, (0, 1, 2)),
    (1152, 384, (1, 2, 0)),
    (1536, 256, (2, 0, 1)),
)
LAST = 5
SETS = ((0, 1, 2), (3, 4, 5))
LAG = 2
FLOW = object()


def coordinates():
    grp = lax.axis_index("grp")
    return lax.axis_index("role"), grp // 8, (grp // 2) % 4, grp % 2


def device(x, z, y, c):
    return {"role": x, "grp": z * 8 + y * 2 + c}


def dot(a, b):
    return jnp.dot(a, b, preferred_element_type=F32)


def onehot(shape, source_of_row):
    rows = lax.broadcasted_iota(jnp.int32, shape, 0)
    columns = lax.broadcasted_iota(jnp.int32, shape, 1)
    return (columns == source_of_row(rows)).astype(BF16)


def kernel(
    len_ref,
    res_ref,
    gain_ref,
    ids_ref,
    gates_ref,
    q_hbm,
    cache_hbm,
    ve_hbm,
    op_hbm,
    wg_hbm,
    wu_hbm,
    wd_hbm,
    out_ref,
    q_buf,
    cache_buf,
    op_buf,
    wg_buf,
    wu_buf,
    wd_buf,
    ve_buf,
    a2a_send,
    a2a_recv,
    gain_f32,
    val_f32,
    val_send,
    val_recv,
    p_refs,
    x_refs,
    y_refs,
    s1_refs,
    r2_refs,
    s2_refs,
    r3_refs,
    n_refs,
    stream_buf,
    acc_g,
    acc_u,
    act_buf,
    far_refs,
    last_send,
    load_sem,
    ve_send_sem,
    ve_recv_sem,
    op_send_sem,
    op_recv_sem,
    a2a_send_sem,
    a2a_recv_sem,
    val_send_sem,
    val_recv_sem,
    rs_send_sem,
    rs_recv_sem,
    ag_send_sem,
    ag_recv_sem,
    pair_send_sem,
    pair_recv_sem,
    far_send_sem,
    far_recv_sem,
    last_send_sem,
    last_recv_sem,
):
    x, z, y, c = coordinates()
    zy = z * 4 + y
    other = 1 - c
    here = (x, z, y)
    me = device(x, z, y, c)
    sibling = device(x, z, y, other)
    sends = []

    def peer(axis, step):
        at = [x, z, y]
        at[axis] = (at[axis] + step) % 4
        return device(at[0], at[1], at[2], c)

    def remote(src, dst, send_sem, recv_sem, to):
        return pltpu.make_async_remote_copy(
            src_ref=src,
            dst_ref=dst,
            send_sem=send_sem,
            recv_sem=recv_sem,
            device_id=to,
            device_id_type=MESH,
        )

    def send(src, dst, send_sem, recv_sem, to):
        copy = remote(src, dst, send_sem, recv_sem, to)
        copy.start()
        sends.append(copy)

    def arrived(dst, send_sem, recv_sem):
        remote(dst, dst, send_sem, recv_sem, me).wait_recv()

    def zy_peer(step):
        p = (zy + step) % 16
        return p, device(x, p // 4, p % 4, c)

    barrier = pltpu.get_barrier_semaphore()

    def greet(step, carry):
        _, to = zy_peer(step)
        pl.semaphore_signal(barrier, inc=1, device_id=to, device_id_type=MESH)
        return carry

    lax.fori_loop(1, 16, greet, 0)
    for step in range(1, 4):
        for core in (c, other):
            pl.semaphore_signal(
                barrier, inc=1, device_id=device((x + step) % 4, z, y, core), device_id_type=MESH
            )
    pl.semaphore_signal(barrier, inc=1, device_id=sibling, device_id_type=MESH)

    ve_own = ve_buf.at[x, :, pl.ds(pl.multiple_of(c * 128, 128), 128)]
    op_own = op_buf.at[pl.ds(pl.multiple_of(c * 128, 128), 128), :]
    load_tokens = []
    for pair in range(2):
        rows = pl.ds(2 * pair, 2)
        load_tokens.append(
            (
                pltpu.make_async_copy(q_hbm.at[0, rows], q_buf.at[rows], load_sem.at[2 * pair]),
                pltpu.make_async_copy(
                    cache_hbm.at[0, rows], cache_buf.at[rows], load_sem.at[2 * pair + 1]
                ),
            )
        )
    load_ve = pltpu.make_async_copy(ve_hbm.at[0], ve_own, load_sem.at[4])
    load_op = pltpu.make_async_copy(op_hbm, op_own, load_sem.at[5])
    load_wg = pltpu.make_async_copy(wg_hbm.at[0], wg_buf, load_sem.at[6])
    load_wu = pltpu.make_async_copy(wu_hbm.at[0], wu_buf, load_sem.at[7])
    load_wd = pltpu.make_async_copy(wd_hbm.at[0], wd_buf, load_sem.at[8])
    for load in (*load_tokens[0], *load_tokens[1], load_ve, load_op):
        load.start()

    gain_f32[...] = gain_ref[...].astype(F32).reshape(1, D)

    order = onehot((128, 128), lambda i: (i % 8) // 2 * 32 + (i // 8) * 2 + i % 2)

    def attend(t):
        query = q_buf[t]
        cache = cache_buf[t]
        scores = (
            lax.dot_general(query, cache, (((0,), (0,)), ((), ())), preferred_element_type=F32)
            * score_scale
        )
        live = lax.broadcasted_iota(jnp.int32, scores.shape, 1) < len_ref[0, t]
        top = jnp.max(jnp.where(live, scores, -1e30), axis=-1, keepdims=True)
        terms = jnp.exp(jnp.where(live, scores - top, -1e30))
        total = jnp.sum(terms, axis=-1, keepdims=True)
        latent = lax.dot_general(
            terms.astype(BF16),
            cache[:512],
            (((1,), (1,)), ((), ())),
            preferred_element_type=F32,
        )
        latent = (latent / total).astype(BF16)
        return dot(order, latent).reshape(16, 8, 512)

    def attend_pair(pair):
        for load in load_tokens[pair]:
            load.wait()
        both = jnp.concatenate([attend(2 * pair), attend(2 * pair + 1)], axis=1)
        a2a_send[pair] = both.astype(BF16)

    def a2a_start(pair):
        def start(step, carry):
            p, to = zy_peer(step)
            remote(
                a2a_send.at[pair, p],
                a2a_recv.at[pair, zy],
                a2a_send_sem.at[pair, step],
                a2a_recv_sem.at[pair, step],
                to,
            ).start()
            return carry

        lax.fori_loop(1, 16, start, 0)
        a2a_recv[pair, zy] = a2a_send[pair, zy]

    def a2a_wait(pair):
        def wait(step, carry):
            p, to = zy_peer(16 - step)
            copy = remote(
                a2a_send.at[pair, zy],
                a2a_recv.at[pair, p],
                a2a_send_sem.at[pair, step],
                a2a_recv_sem.at[pair, step],
                to,
            )
            copy.wait_send()
            copy.wait_recv()
            return carry

        lax.fori_loop(1, 16, wait, 0)

    attend_pair(0)
    for load in (load_wg, load_wu, load_wd):
        load.start()
    pl.semaphore_wait(barrier, 22)
    a2a_start(0)

    load_ve.wait()
    for step in range(1, 4):
        send(
            ve_own,
            ve_own,
            ve_send_sem.at[step],
            ve_recv_sem.at[step],
            device((x + step) % 4, z, y, c),
        )
    load_op.wait()
    send(op_own, op_own, op_send_sem.at[0], op_recv_sem.at[0], sibling)

    attend_pair(1)
    a2a_start(1)
    for step in range(1, 4):
        arrived(
            ve_buf.at[(x + 4 - step) % 4, :, pl.ds(pl.multiple_of(c * 128, 128), 128)],
            ve_send_sem.at[step],
            ve_recv_sem.at[step],
        )
    ve_ring = ve_buf.at[:, :, pl.ds(pl.multiple_of(c * 128, 128), 128)]
    send(ve_ring, ve_ring, ve_send_sem.at[0], ve_recv_sem.at[0], sibling)
    a2a_wait(0)
    a2a_wait(1)
    arrived(
        ve_buf.at[:, :, pl.ds(pl.multiple_of(other * 128, 128), 128)],
        ve_send_sem.at[0],
        ve_recv_sem.at[0],
    )

    latents = a2a_recv[...].reshape(512, 512)
    head_of_row = lax.broadcasted_iota(jnp.int32, (512, 128), 0) % 8
    values = jnp.zeros((512, 128), F32)
    for h in range(4):
        product = dot(latents, ve_buf[h])
        values = jnp.where(head_of_row == 2 * h, product[:, :128], values)
        values = jnp.where(head_of_row == 2 * h + 1, product[:, 128:], values)
    val_f32[...] = values
    for h in range(4):
        val_send[h] = jnp.concatenate(
            [val_f32[pl.ds(2 * h, 64, stride=8), :], val_f32[pl.ds(2 * h + 1, 64, stride=8), :]],
            axis=1,
        ).astype(BF16)
    for step in range(1, 4):
        to = (x + step) % 4
        send(
            val_send.at[to],
            val_recv.at[x],
            val_send_sem.at[step],
            val_recv_sem.at[step],
            device(to, z, y, c),
        )
    val_recv[x] = val_send[x]
    arrived(
        op_buf.at[pl.ds(pl.multiple_of(other * 128, 128), 128), :],
        op_send_sem.at[0],
        op_recv_sem.at[0],
    )
    for step in range(1, 4):
        arrived(val_recv.at[(x + 4 - step) % 4], val_send_sem.at[step], val_recv_sem.at[step])

    token_order = onehot((256, 256), lambda i: (i % 16) // 4 * 64 + (i % 4) // 2 * 32 + (i // 16) * 2 + i % 2)
    rows = dot(token_order, val_recv[...].reshape(256, 256)).astype(BF16)

    own_rows = onehot((16, 4), lambda i: jnp.where(i // 4 == x, i % 4, -1))

    halves = (pl.ds(0, 2), pl.ds(2, 2))

    def ring_block(flow, index, half):
        at = [slice(None)] * 3
        first = FLOWS[flow][2][0]
        at[first] = index
        if half is not None:
            at[1 if first == 0 else 0] = halves[half]
        return tuple(at)

    def rs_sem(round_, flow, k):
        s = (round_ * 6 + flow) * 12 + k
        return rs_send_sem.at[s], rs_recv_sem.at[s]

    def ring_at(flow, step):
        return (here[FLOWS[flow][2][0]] + step) % 4

    def ring_start(round_, flow):
        axis = FLOWS[flow][2][0]
        p = p_refs[flow]
        for k, (step, block, half) in enumerate(((1, 2, 0), (3, 2, 1))):
            send(
                p.at[ring_block(flow, ring_at(flow, block), half)],
                x_refs[flow].at[k],
                *rs_sem(round_, flow, k),
                peer(axis, step),
            )
        for k, (step, half) in enumerate(((1, 1), (3, 0))):
            send(
                p.at[ring_block(flow, ring_at(flow, step), half)],
                y_refs[flow].at[k, halves[half]],
                *rs_sem(round_, flow, 2 + k),
                peer(axis, step),
            )

    def ring_pass(round_, flow):
        axis = FLOWS[flow][2][0]
        p = p_refs[flow]
        for k, (step, half) in enumerate(((1, 0), (3, 1))):
            arrived(x_refs[flow].at[k], *rs_sem(round_, flow, k))
            own = p.at[ring_block(flow, ring_at(flow, step), half)]

            def add(i, carry, own=own, k=k):
                own[i] = (own[i].astype(F32) + x_refs[flow][k, i].astype(F32)).astype(BF16)
                return carry

            lax.fori_loop(0, 2, add, 0)
            send(
                own,
                y_refs[flow].at[k, halves[half]],
                *rs_sem(round_, flow, 4 + k),
                peer(axis, step),
            )

    def ring_end(round_, flow):
        for k, half in ((0, 1), (1, 0)):
            arrived(y_refs[flow].at[k, halves[half]], *rs_sem(round_, flow, 2 + k))
        for k, half in ((0, 0), (1, 1)):
            arrived(y_refs[flow].at[k, halves[half]], *rs_sem(round_, flow, 4 + k))
        own = p_refs[flow].at[ring_block(flow, ring_at(flow, 0), None)]
        y_ref = y_refs[flow]

        def add(i, carry):
            total = own[i].astype(F32) + y_ref[0, i].astype(F32) + y_ref[1, i].astype(F32)
            s1_refs[flow][i] = total.astype(BF16)
            return carry

        lax.fori_loop(0, 4, add, 0)
        direct_start(round_, flow, 1)

    def direct_block(flow, phase, index):
        if phase == 2:
            return s2_refs[flow].at[index]
        _, axis, last = FLOWS[flow][2]
        return s1_refs[flow].at[(index,) if axis < last else (slice(None), index)]

    def direct_start(round_, flow, phase):
        axis = FLOWS[flow][2][phase]
        received = (r2_refs if phase == 1 else r3_refs)[flow]
        for step in range(1, 4):
            send(
                direct_block(flow, phase, (here[axis] + step) % 4),
                received.at[step - 1],
                *rs_sem(round_, flow, 3 + 3 * phase + step - 1),
                peer(axis, step),
            )

    def direct_end(round_, flow, phase):
        axis = FLOWS[flow][2][phase]
        received = (r2_refs if phase == 1 else r3_refs)[flow]
        for step in range(1, 4):
            arrived(received.at[step - 1], *rs_sem(round_, flow, 3 + 3 * phase + step - 1))
        total = direct_block(flow, phase, here[axis])[...].astype(F32)
        for k in range(3):
            total = total + received[k].astype(F32)
        if phase == 2:
            return total
        s2_refs[flow][...] = total.astype(BF16)
        direct_start(round_, flow, 2)
        return None

    def project(flow):
        offset, width, _ = FLOWS[flow]

        def chunk(k, carry):
            columns = pl.ds(pl.multiple_of(k * QUARTER + offset, 128), width)
            p_refs[flow][k] = dot(rows, op_buf[:, columns]).astype(BF16).reshape(4, 4, 16, width)
            own = p_refs[flow].at[k, z, y]
            own[...] = (own[...].astype(F32) + dot(own_rows, res_ref[:, columns])).astype(BF16)
            return carry

        lax.fori_loop(0, 4, chunk, 0)
        ring_start(0, flow)

    squares = []

    def keep_stream(flow):
        offset, width, _ = FLOWS[flow]
        result = direct_end(0, flow, 2)
        stream_buf[:, offset : offset + width] = result
        squares.append(jnp.sum(result * result, axis=-1, keepdims=True))
        columns = pl.ds(pl.multiple_of(x * QUARTER + offset, 128), width)
        n_refs[flow][c, x, z, y, :, :width] = (result * gain_f32[:, columns]).astype(BF16)
        if flow == LAST:
            lane = lax.broadcasted_iota(jnp.int32, (4, 128), 1)
            table = jnp.zeros((4, 128), F32)
            gates = gates_ref[...].astype(F32)
            for k in range(8):
                table = table + jnp.where(ids_ref[:, k : k + 1] == lane, gates[:, k : k + 1], 0.0)
            table = dot(own_rows, table.astype(BF16))
            square = sum(squares)
            high = square.astype(BF16).astype(F32)
            lane16 = lax.broadcasted_iota(jnp.int32, (16, 128), 1)
            extra = jnp.where(lane16 == 32, high, jnp.where(lane16 == 33, square - high, table))
            n_refs[flow][c, x, z, y, :, width:] = extra.astype(BF16)
        ag_start(flow, 2)

    def ag_sem(flow, k):
        s = flow * 12 + k
        return ag_send_sem.at[s], ag_recv_sem.at[s]

    def ag_block(flow, phase, index):
        axes = FLOWS[flow][2]
        at = [slice(None)] * 3
        for a in axes[:phase]:
            at[a] = here[a]
        at[axes[phase]] = index
        return n_refs[flow].at[(c, *at)]

    def ag_start(flow, phase):
        axis = FLOWS[flow][2][phase]
        own = ag_block(flow, phase, here[axis])
        for step in range(1, 4):
            send(own, own, *ag_sem(flow, 3 + 3 * phase + step - 1), peer(axis, step))

    def ag_end(flow, phase):
        axis = FLOWS[flow][2][phase]
        for step in range(1, 4):
            arrived(
                ag_block(flow, phase, (here[axis] + 4 - step) % 4),
                *ag_sem(flow, 3 + 3 * phase + step - 1),
            )
        if phase == 2:
            ag_start(flow, 1)
        else:
            for k, (step, half) in enumerate(((1, 0), (3, 1), (1, 1), (3, 0))):
                own = n_refs[flow].at[(c, *ring_block(flow, ring_at(flow, 0), half))]
                send(own, own, *ag_sem(flow, k), peer(FLOWS[flow][2][0], step))

    def ag_pass(flow):
        for k, (step, half) in enumerate(((1, 0), (3, 1))):
            got = n_refs[flow].at[(c, *ring_block(flow, ring_at(flow, 4 - step), half))]
            arrived(got, *ag_sem(flow, k))
            send(got, got, *ag_sem(flow, 4 + k), peer(FLOWS[flow][2][0], step))

    def ag_last(flow):
        for k, (step, half) in enumerate(((1, 1), (3, 0))):
            got = n_refs[flow].at[(c, *ring_block(flow, ring_at(flow, 4 - step), half))]
            arrived(got, *ag_sem(flow, 2 + k))
        for k, half in enumerate((0, 1)):
            got = n_refs[flow].at[(c, *ring_block(flow, ring_at(flow, 2), half))]
            arrived(got, *ag_sem(flow, 4 + k))
        half = n_refs[flow].at[c]
        send(half, half, pair_send_sem.at[flow], pair_recv_sem.at[flow], sibling)

    def up(flow, half):
        offset, width, _ = FLOWS[flow]
        core = (c, other)[half]
        if half == 1:
            arrived(n_refs[flow].at[core], pair_send_sem.at[flow], pair_recv_sem.at[flow])
        if flow == 0:
            if half == 0:
                load_wg.wait()
                load_wu.wait()
            acc_g[half] = jnp.zeros((256, 512), F32)
            acc_u[half] = jnp.zeros((256, 512), F32)

        def chunk(k, carry):
            rows = n_refs[flow][core, k, :, :, :, :width].reshape(256, width)
            depth = pl.ds(pl.multiple_of(k * QUARTER + offset, 128), width)
            acc_g[half] += dot(rows, wg_buf[depth, :])
            acc_u[half] += dot(rows, wu_buf[depth, :])
            return carry

        lax.fori_loop(0, 4, chunk, 0)

    expert = z * 8 + y * 2 + c
    lanes = lax.broadcasted_iota(jnp.int32, (256, 128), 1)

    def activate(half):
        core = (c, other)[half]
        extra = jnp.zeros((256, 128), F32)
        for k in range(4):
            extra = extra + n_refs[LAST][core, k, :, :, :, 256:].reshape(256, 128).astype(F32)
        weight = jnp.sum(jnp.where(lanes == expert, extra, 0.0), axis=-1, keepdims=True)
        square = jnp.sum(
            jnp.where((lanes == 32) | (lanes == 33), extra, 0.0), axis=-1, keepdims=True
        )
        scale = lax.rsqrt(square * (1.0 / D) + norm_eps)
        gate = acc_g[half] * scale
        act = gate / (1.0 + jnp.exp(-gate)) * (acc_u[half] * scale)
        act_buf[half] = (act * weight).astype(BF16)

    def each(function, *arguments):
        def run(number):
            for flow in SETS[number]:
                function(*(flow if a is FLOW else a for a in arguments))

        return run

    first = (
        each(project, FLOW),
        each(ring_pass, 0, FLOW),
        each(ring_end, 0, FLOW),
        each(direct_end, 0, FLOW, 1),
        each(keep_stream, FLOW),
        each(ag_end, FLOW, 2),
        each(ag_end, FLOW, 1),
        each(ag_pass, FLOW),
        each(ag_last, FLOW),
        each(up, FLOW, 0),
        each(up, FLOW, 1),
    )
    for tick in range(len(first) + LAG):
        if tick < len(first):
            first[tick](0)
        if tick >= LAG:
            first[tick - LAG](1)
    activate(1)
    activate(0)

    for copy in sends:
        copy.wait_send()
    sends.clear()

    load_wd.wait()

    def down_far(flow):
        offset, width, _ = FLOWS[flow]

        def chunk(k, carry):
            columns = pl.ds(pl.multiple_of(k * QUARTER + offset, 128), width)
            n_refs[flow][c, k, :, :, :, :width] = (
                dot(act_buf[1], wd_buf[:, columns]).astype(BF16).reshape(4, 4, 16, width)
            )
            return carry

        lax.fori_loop(0, 4, chunk, 0)
        send(
            n_refs[flow].at[c, :, :, :, :, pl.ds(0, width)],
            far_refs[flow],
            far_send_sem.at[flow],
            far_recv_sem.at[flow],
            sibling,
        )

    def down_near(flow):
        offset, width, _ = FLOWS[flow]
        arrived(far_refs[flow], far_send_sem.at[flow], far_recv_sem.at[flow])

        def chunk(k, carry):
            columns = pl.ds(pl.multiple_of(k * QUARTER + offset, 128), width)
            total = dot(act_buf[0], wd_buf[:, columns])
            total = total + far_refs[flow][k].reshape(256, width).astype(F32)
            p_refs[flow][k] = total.astype(BF16).reshape(4, 4, 16, width)
            return carry

        lax.fori_loop(0, 4, chunk, 0)
        ring_start(1, flow)

    def add_stream(flow):
        offset, width, _ = FLOWS[flow]
        stream_buf[:, offset : offset + width] += direct_end(1, flow, 2)

    down_far(0)
    for flow in range(6):
        if flow < 5:
            down_far(flow + 1)
        down_near(flow)
        if flow == 4:
            each(ring_pass, 1, FLOW)(0)
    second = (
        each(ring_end, 1, FLOW),
        each(direct_end, 1, FLOW, 1),
        each(add_stream, FLOW),
    )
    each(ring_pass, 1, FLOW)(1)
    for stage in second:
        stage(0)
        stage(1)

    rounded = stream_buf[...].astype(BF16)
    last = jnp.zeros((64, 512), F32)
    for j in range(4):
        pick = onehot(
            (64, 16), lambda i: jnp.where((i % 16) // 4 == j, i // 16 * 4 + i % 4, -1)
        )
        piece = rounded[:, j * 512 : min(j * 512 + 512, QUARTER)]
        moved = dot(pick, piece)
        if moved.shape[1] < 512:
            moved = jnp.concatenate([moved, jnp.zeros((64, 512 - moved.shape[1]), F32)], axis=1)
        last = last + moved
    last_send[...] = last.astype(BF16).reshape(4, 16, 512)
    for step in range(1, 4):
        to = (x + step) % 4
        send(
            last_send.at[to],
            out_ref.at[x],
            last_send_sem.at[step],
            last_recv_sem.at[step],
            device(to, z, y, c),
        )
    out_ref[x] = last_send[x]
    for step in range(1, 4):
        arrived(out_ref.at[(x + 4 - step) % 4], last_send_sem.at[step], last_recv_sem.at[step])
    for copy in sends:
        copy.wait_send()


def per_device(
    queries,
    compressed_cache,
    lengths,
    value_expand_matrix,
    out_proj,
    residual,
    norm_gain,
    expert_ids,
    expert_gates,
    w_gate,
    w_up,
    w_down,
):
    vmem = lambda *shape, dtype=BF16: pltpu.VMEM(shape, dtype)
    widths = [w for _, w, _ in FLOWS]
    dma = lambda *n: pltpu.SemaphoreType.DMA(n)
    scratch = [
        vmem(4, 576, 128),
        vmem(4, 576, 512),
        vmem(256, D),
        vmem(D, 512),
        vmem(D, 512),
        vmem(512, D),
        vmem(4, 512, 256),
        vmem(2, 16, 16, 512),
        vmem(2, 16, 16, 512),
        vmem(1, D, dtype=F32),
        vmem(512, 128, dtype=F32),
        vmem(4, 64, 256),
        vmem(4, 64, 256),
        tuple(vmem(4, 4, 4, 16, w) for w in widths),
        tuple(vmem(2, 2, 4, 16, w) for w in widths),
        tuple(vmem(2, 4, 4, 16, w) for w in widths),
        tuple(vmem(4, 4, 16, w) for w in widths),
        tuple(vmem(3, 4, 16, w) for w in widths),
        tuple(vmem(4, 16, w) for w in widths),
        tuple(vmem(3, 16, w) for w in widths),
        tuple(vmem(2, 4, 4, 4, 16, w + 128 * (f == LAST)) for f, w in enumerate(widths)),
        vmem(16, QUARTER, dtype=F32),
        vmem(2, 256, 512, dtype=F32),
        vmem(2, 256, 512, dtype=F32),
        vmem(2, 256, 512),
        tuple(vmem(4, 4, 4, 16, w) for w in widths),
        vmem(4, 16, 512),
        dma(9),
        dma(4),
        dma(4),
        dma(1),
        dma(1),
        dma(2, 16),
        dma(2, 16),
        dma(4),
        dma(4),
        dma(144),
        dma(144),
        dma(72),
        dma(72),
        dma(6),
        dma(6),
        dma(6),
        dma(6),
        dma(4),
        dma(4),
    ]
    in_vmem = pl.BlockSpec(memory_space=pltpu.VMEM)
    anywhere = pl.BlockSpec(memory_space=pl.ANY)
    result = pl.pallas_call(
        kernel,
        out_shape=jax.ShapeDtypeStruct((4, 16, 512), BF16),
        in_specs=[pl.BlockSpec(memory_space=pltpu.SMEM)] + [in_vmem] * 4 + [anywhere] * 7,
        out_specs=in_vmem,
        scratch_shapes=scratch,
        compiler_params=pltpu.CompilerParams(
            collective_id=0, has_side_effects=True, vmem_limit_bytes=64 << 20
        ),
        cost_estimate=pl.CostEstimate(
            flops=14 * 10**9, bytes_accessed=28 * 10**6, transcendentals=600_000
        ),
        name="layer",
    )(
        lengths,
        residual[0],
        norm_gain,
        expert_ids[0],
        expert_gates[0],
        jnp.swapaxes(queries, 2, 3),
        jnp.swapaxes(compressed_cache, 2, 3),
        value_expand_matrix,
        out_proj,
        w_gate,
        w_up,
        w_down,
    )
    result = result.reshape(4, 4, 4, 512).transpose(2, 0, 1, 3).reshape(4, 4, 2048)
    return result[:, :, :QUARTER].reshape(1, 4, D)


def solution(mesh):
    in_specs = (
        P("grp", "role", None, None),
        P("grp", "role", None, None),
        P("grp", "role"),
        P(("role", "grp"), None, None),
        P(("role", "grp"), None),
        P("grp", "role", None),
        P(),
        P("grp", "role", None),
        P("grp", "role", None),
        P("grp", None, "role"),
        P("grp", None, "role"),
        P("grp", "role", None),
    )
    out_specs = P("grp", "role", None)
    return jax.shard_map(
        per_device, mesh=mesh, in_specs=in_specs, out_specs=out_specs, check_vma=False
    )
```

```python
import jax
import jax.numpy as jnp
from jax import lax
from jax.experimental import pallas as pl
from jax.experimental.pallas import tpu as pltpu
from jax.sharding import PartitionSpec as P

MESH = pl.DeviceIdType.MESH
F32 = jnp.float32
BF16 = jnp.bfloat16

score_scale = 192.0 ** (-0.5)
norm_eps = 1e-06

D = 7168
QUARTER = 1792
FLOWS = (
    (0, 384, (0, 1, 2)),
    (384, 256, (1, 2, 0)),
    (640, 256, (2, 0, 1)),
    (896, 256, (0, 1, 2)),
    (1152, 384, (1, 2, 0)),
    (1536, 256, (2, 0, 1)),
)
LAST = 5
SETS = ((0, 1, 2), (3, 4, 5))
FIRST_ORDER = tuple((stage, number) for stage in range(6) for number in (0, 1)) + (
    (6, 0),
    (7, 0),
    (6, 1),
    (8, 0),
    (9, 0),
    (7, 1),
    (10, 0),
    (8, 1),
    (9, 1),
    (10, 1),
)
FLOW = object()


def coordinates():
    grp = lax.axis_index("grp")
    return lax.axis_index("role"), grp // 8, (grp // 2) % 4, grp % 2


def device(x, z, y, c):
    return {"role": x, "grp": z * 8 + y * 2 + c}


def dot(a, b):
    return jnp.dot(a, b, preferred_element_type=F32)


def onehot(shape, source_of_row):
    rows = lax.broadcasted_iota(jnp.int32, shape, 0)
    columns = lax.broadcasted_iota(jnp.int32, shape, 1)
    return (columns == source_of_row(rows)).astype(BF16)


def kernel(
    len_ref,
    res_ref,
    gain_ref,
    ids_ref,
    gates_ref,
    q_hbm,
    cache_hbm,
    ve_hbm,
    op_hbm,
    wg_hbm,
    wu_hbm,
    wd_hbm,
    out_ref,
    q_buf,
    cache_buf,
    op_buf,
    wg_buf,
    wu_buf,
    wd_buf,
    ve_buf,
    a2a_send,
    a2a_recv,
    gain_f32,
    val_f32,
    val_send,
    val_recv,
    p_refs,
    x_refs,
    y_refs,
    s1_refs,
    r2_refs,
    s2_refs,
    r3_refs,
    n_refs,
    stream_buf,
    acc_g,
    acc_u,
    act_buf,
    far_refs,
    last_send,
    last_recv,
    load_sem,
    ve_send_sem,
    ve_recv_sem,
    op_send_sem,
    op_recv_sem,
    a2a_send_sem,
    a2a_recv_sem,
    val_send_sem,
    val_recv_sem,
    rs_send_sem,
    rs_recv_sem,
    ag_send_sem,
    ag_recv_sem,
    pair_send_sem,
    pair_recv_sem,
    far_send_sem,
    far_recv_sem,
    last_send_sem,
    last_recv_sem,
):
    x, z, y, c = coordinates()
    zy = z * 4 + y
    other = 1 - c
    here = (x, z, y)
    me = device(x, z, y, c)
    sibling = device(x, z, y, other)
    sends = []

    def peer(axis, step):
        at = [x, z, y]
        at[axis] = (at[axis] + step) % 4
        return device(at[0], at[1], at[2], c)

    def remote(src, dst, send_sem, recv_sem, to):
        return pltpu.make_async_remote_copy(
            src_ref=src,
            dst_ref=dst,
            send_sem=send_sem,
            recv_sem=recv_sem,
            device_id=to,
            device_id_type=MESH,
        )

    def send(src, dst, send_sem, recv_sem, to):
        copy = remote(src, dst, send_sem, recv_sem, to)
        copy.start()
        sends.append(copy)

    def arrived(dst, send_sem, recv_sem):
        remote(dst, dst, send_sem, recv_sem, me).wait_recv()

    def zy_peer(step):
        p = (zy + step) % 16
        return p, device(x, p // 4, p % 4, c)

    barrier = pltpu.get_barrier_semaphore()

    def greet(step, carry):
        _, to = zy_peer(step)
        pl.semaphore_signal(barrier, inc=1, device_id=to, device_id_type=MESH)
        return carry

    lax.fori_loop(1, 16, greet, 0)
    for step in range(1, 4):
        for core in (c, other):
            pl.semaphore_signal(
                barrier, inc=1, device_id=device((x + step) % 4, z, y, core), device_id_type=MESH
            )
    pl.semaphore_signal(barrier, inc=1, device_id=sibling, device_id_type=MESH)

    ve_own = ve_buf.at[x, :, pl.ds(pl.multiple_of(c * 128, 128), 128)]
    op_own = op_buf.at[pl.ds(pl.multiple_of(c * 128, 128), 128), :]
    load_tokens = []
    for pair in range(2):
        rows = pl.ds(2 * pair, 2)
        load_tokens.append(
            (
                pltpu.make_async_copy(q_hbm.at[0, rows], q_buf.at[rows], load_sem.at[2 * pair]),
                pltpu.make_async_copy(
                    cache_hbm.at[0, rows], cache_buf.at[rows], load_sem.at[2 * pair + 1]
                ),
            )
        )
    load_ve = pltpu.make_async_copy(ve_hbm.at[0], ve_own, load_sem.at[4])
    load_op = pltpu.make_async_copy(op_hbm, op_own, load_sem.at[5])
    load_wg = pltpu.make_async_copy(wg_hbm.at[0], wg_buf, load_sem.at[6])
    load_wu = pltpu.make_async_copy(wu_hbm.at[0], wu_buf, load_sem.at[7])
    load_wd = pltpu.make_async_copy(wd_hbm.at[0], wd_buf, load_sem.at[8])
    for load in (*load_tokens[0], *load_tokens[1], load_ve, load_op):
        load.start()

    gain_f32[...] = gain_ref[...].astype(F32).reshape(1, D)

    order = onehot((128, 128), lambda i: (i % 8) // 2 * 32 + (i // 8) * 2 + i % 2)

    def attend(t):
        query = q_buf[t]
        cache = cache_buf[t]
        scores = (
            lax.dot_general(query, cache, (((0,), (0,)), ((), ())), preferred_element_type=F32)
            * score_scale
        )
        live = lax.broadcasted_iota(jnp.int32, scores.shape, 1) < len_ref[0, t]
        top = jnp.max(jnp.where(live, scores, -1e30), axis=-1, keepdims=True)
        terms = jnp.exp(jnp.where(live, scores - top, -1e30))
        total = jnp.sum(terms, axis=-1, keepdims=True)
        latent = lax.dot_general(
            terms.astype(BF16),
            cache[:512],
            (((1,), (1,)), ((), ())),
            preferred_element_type=F32,
        )
        latent = (latent / total).astype(BF16)
        return dot(order, latent).reshape(16, 8, 512)

    def attend_pair(pair):
        for load in load_tokens[pair]:
            load.wait()
        both = jnp.concatenate([attend(2 * pair), attend(2 * pair + 1)], axis=1)
        a2a_send[pair] = both.astype(BF16)

    def a2a_start(pair):
        for step in range(1, 16):
            p, to = zy_peer(step)
            remote(
                a2a_send.at[pair, p],
                a2a_recv.at[pair, zy],
                a2a_send_sem.at[pair, step],
                a2a_recv_sem.at[pair, step],
                to,
            ).start()
        a2a_recv[pair, zy] = a2a_send[pair, zy]

    def a2a_wait(pair):
        for step in range(1, 16):
            p, to = zy_peer(16 - step)
            copy = remote(
                a2a_send.at[pair, zy],
                a2a_recv.at[pair, p],
                a2a_send_sem.at[pair, step],
                a2a_recv_sem.at[pair, step],
                to,
            )
            copy.wait_send()
            copy.wait_recv()

    attend_pair(0)
    for load in (load_wg, load_wu, load_wd):
        load.start()
    pl.semaphore_wait(barrier, 22)
    a2a_start(0)

    load_ve.wait()
    for step in range(1, 4):
        send(
            ve_own,
            ve_own,
            ve_send_sem.at[step],
            ve_recv_sem.at[step],
            device((x + step) % 4, z, y, c),
        )
    load_op.wait()
    send(op_own, op_own, op_send_sem.at[0], op_recv_sem.at[0], sibling)

    attend_pair(1)
    a2a_start(1)
    for step in range(1, 4):
        arrived(
            ve_buf.at[(x + 4 - step) % 4, :, pl.ds(pl.multiple_of(c * 128, 128), 128)],
            ve_send_sem.at[step],
            ve_recv_sem.at[step],
        )
    ve_ring = ve_buf.at[:, :, pl.ds(pl.multiple_of(c * 128, 128), 128)]
    send(ve_ring, ve_ring, ve_send_sem.at[0], ve_recv_sem.at[0], sibling)
    a2a_wait(0)
    a2a_wait(1)
    arrived(
        ve_buf.at[:, :, pl.ds(pl.multiple_of(other * 128, 128), 128)],
        ve_send_sem.at[0],
        ve_recv_sem.at[0],
    )

    latents = a2a_recv[...].reshape(512, 512)
    head_of_row = lax.broadcasted_iota(jnp.int32, (512, 128), 0) % 8
    values = jnp.zeros((512, 128), F32)
    for h in range(4):
        product = dot(latents, ve_buf[h])
        values = jnp.where(head_of_row == 2 * h, product[:, :128], values)
        values = jnp.where(head_of_row == 2 * h + 1, product[:, 128:], values)
    val_f32[...] = values
    for h in range(4):
        val_send[h] = jnp.concatenate(
            [val_f32[pl.ds(2 * h, 64, stride=8), :], val_f32[pl.ds(2 * h + 1, 64, stride=8), :]],
            axis=1,
        ).astype(BF16)
    for step in range(1, 4):
        to = (x + step) % 4
        send(
            val_send.at[to],
            val_recv.at[x],
            val_send_sem.at[step],
            val_recv_sem.at[step],
            device(to, z, y, c),
        )
    val_recv[x] = val_send[x]
    arrived(
        op_buf.at[pl.ds(pl.multiple_of(other * 128, 128), 128), :],
        op_send_sem.at[0],
        op_recv_sem.at[0],
    )
    for step in range(1, 4):
        arrived(val_recv.at[(x + 4 - step) % 4], val_send_sem.at[step], val_recv_sem.at[step])

    token_order = onehot((256, 256), lambda i: (i % 16) // 4 * 64 + (i % 4) // 2 * 32 + (i // 16) * 2 + i % 2)
    rows = dot(token_order, val_recv[...].reshape(256, 256)).astype(BF16)

    own_rows = onehot((16, 4), lambda i: jnp.where(i // 4 == x, i % 4, -1))

    halves = (pl.ds(0, 2), pl.ds(2, 2))

    def ring_block(flow, index, half):
        at = [slice(None)] * 3
        first = FLOWS[flow][2][0]
        at[first] = index
        if half is not None:
            at[1 if first == 0 else 0] = halves[half]
        return tuple(at)

    def rs_sem(round_, flow, k):
        s = (round_ * 6 + flow) * 12 + k
        return rs_send_sem.at[s], rs_recv_sem.at[s]

    def ring_at(flow, step):
        return (here[FLOWS[flow][2][0]] + step) % 4

    def ring_start(round_, flow):
        axis = FLOWS[flow][2][0]
        p = p_refs[flow]
        for k, (step, block, half) in enumerate(((1, 2, 0), (3, 2, 1))):
            send(
                p.at[ring_block(flow, ring_at(flow, block), half)],
                x_refs[flow].at[k],
                *rs_sem(round_, flow, k),
                peer(axis, step),
            )
        for k, (step, half) in enumerate(((1, 1), (3, 0))):
            send(
                p.at[ring_block(flow, ring_at(flow, step), half)],
                y_refs[flow].at[k, halves[half]],
                *rs_sem(round_, flow, 2 + k),
                peer(axis, step),
            )

    def ring_pass(round_, flow):
        axis = FLOWS[flow][2][0]
        p = p_refs[flow]
        for k, (step, half) in enumerate(((1, 0), (3, 1))):
            arrived(x_refs[flow].at[k], *rs_sem(round_, flow, k))
            own = p.at[ring_block(flow, ring_at(flow, step), half)]
            own[...] = (own[...].astype(F32) + x_refs[flow][k].astype(F32)).astype(BF16)
            send(
                own,
                y_refs[flow].at[k, halves[half]],
                *rs_sem(round_, flow, 4 + k),
                peer(axis, step),
            )

    def ring_end(round_, flow):
        for k, half in ((0, 1), (1, 0)):
            arrived(y_refs[flow].at[k, halves[half]], *rs_sem(round_, flow, 2 + k))
        for k, half in ((0, 0), (1, 1)):
            arrived(y_refs[flow].at[k, halves[half]], *rs_sem(round_, flow, 4 + k))
        own = p_refs[flow].at[ring_block(flow, ring_at(flow, 0), None)]
        y_ref = y_refs[flow]
        total = own[...].astype(F32) + y_ref[0].astype(F32) + y_ref[1].astype(F32)
        s1_refs[flow][...] = total.astype(BF16)
        direct_start(round_, flow, 1)

    def direct_block(flow, phase, index):
        if phase == 2:
            return s2_refs[flow].at[index]
        _, axis, last = FLOWS[flow][2]
        return s1_refs[flow].at[(index,) if axis < last else (slice(None), index)]

    def direct_start(round_, flow, phase):
        axis = FLOWS[flow][2][phase]
        received = (r2_refs if phase == 1 else r3_refs)[flow]
        for step in range(1, 4):
            send(
                direct_block(flow, phase, (here[axis] + step) % 4),
                received.at[step - 1],
                *rs_sem(round_, flow, 3 + 3 * phase + step - 1),
                peer(axis, step),
            )

    def direct_end(round_, flow, phase):
        axis = FLOWS[flow][2][phase]
        received = (r2_refs if phase == 1 else r3_refs)[flow]
        for step in range(1, 4):
            arrived(received.at[step - 1], *rs_sem(round_, flow, 3 + 3 * phase + step - 1))
        total = direct_block(flow, phase, here[axis])[...].astype(F32)
        for k in range(3):
            total = total + received[k].astype(F32)
        if phase == 2:
            return total
        s2_refs[flow][...] = total.astype(BF16)
        direct_start(round_, flow, 2)
        return None

    def project(flow):
        offset, width, _ = FLOWS[flow]

        for k in range(4):
            columns = slice(k * QUARTER + offset, k * QUARTER + offset + width)
            p_refs[flow][k] = dot(rows, op_buf[:, columns]).astype(BF16).reshape(4, 4, 16, width)
            own = p_refs[flow].at[k, z, y]
            own[...] = (own[...].astype(F32) + dot(own_rows, res_ref[:, columns])).astype(BF16)
        ring_start(0, flow)

    squares = []

    def keep_stream(flow):
        offset, width, _ = FLOWS[flow]
        result = direct_end(0, flow, 2)
        stream_buf[:, offset : offset + width] = result
        squares.append(jnp.sum(result * result, axis=-1, keepdims=True))
        columns = pl.ds(pl.multiple_of(x * QUARTER + offset, 128), width)
        n_refs[flow][c, x, z, y, :, :width] = (result * gain_f32[:, columns]).astype(BF16)
        if flow == LAST:
            lane = lax.broadcasted_iota(jnp.int32, (4, 128), 1)
            table = jnp.zeros((4, 128), F32)
            gates = gates_ref[...].astype(F32)
            for k in range(8):
                table = table + jnp.where(ids_ref[:, k : k + 1] == lane, gates[:, k : k + 1], 0.0)
            table = dot(own_rows, table.astype(BF16))
            square = sum(squares)
            high = square.astype(BF16).astype(F32)
            lane16 = lax.broadcasted_iota(jnp.int32, (16, 128), 1)
            extra = jnp.where(lane16 == 32, high, jnp.where(lane16 == 33, square - high, table))
            n_refs[flow][c, x, z, y, :, width:] = extra.astype(BF16)
        ag_start(flow, 2)

    def ag_sem(flow, k):
        s = flow * 12 + k
        return ag_send_sem.at[s], ag_recv_sem.at[s]

    def ag_block(flow, phase, index):
        axes = FLOWS[flow][2]
        at = [slice(None)] * 3
        for a in axes[:phase]:
            at[a] = here[a]
        at[axes[phase]] = index
        return n_refs[flow].at[(c, *at)]

    def ag_start(flow, phase):
        axis = FLOWS[flow][2][phase]
        own = ag_block(flow, phase, here[axis])
        for step in range(1, 4):
            send(own, own, *ag_sem(flow, 3 + 3 * phase + step - 1), peer(axis, step))

    def ag_end(flow, phase):
        axis = FLOWS[flow][2][phase]
        for step in range(1, 4):
            arrived(
                ag_block(flow, phase, (here[axis] + 4 - step) % 4),
                *ag_sem(flow, 3 + 3 * phase + step - 1),
            )
        if phase == 2:
            ag_start(flow, 1)
        else:
            for k, (step, half) in enumerate(((1, 0), (3, 1), (1, 1), (3, 0))):
                own = n_refs[flow].at[(c, *ring_block(flow, ring_at(flow, 0), half))]
                send(own, own, *ag_sem(flow, k), peer(FLOWS[flow][2][0], step))
            pair_pieces(flow, c, (0,))

    def pair_piece(flow, core, k, index, half):
        piece = n_refs[flow].at[(core, *ring_block(flow, index, half))]
        s = flow * 6 + k
        if core is c:
            send(piece, piece, pair_send_sem.at[s], pair_recv_sem.at[s], sibling)
        else:
            arrived(piece, pair_send_sem.at[s], pair_recv_sem.at[s])

    pieces = ((0, None), (3, 0), (1, 1), (3, 1), (1, 0), (2, None))

    def pair_pieces(flow, core, numbers):
        for k in numbers:
            step, half = pieces[k]
            pair_piece(flow, core, k, ring_at(flow, step), half)

    def ag_pass(flow):
        for k, (step, half) in enumerate(((1, 0), (3, 1))):
            got = n_refs[flow].at[(c, *ring_block(flow, ring_at(flow, 4 - step), half))]
            arrived(got, *ag_sem(flow, k))
            send(got, got, *ag_sem(flow, 4 + k), peer(FLOWS[flow][2][0], step))
        pair_pieces(flow, c, (1, 2))

    def ag_last(flow):
        for k, (step, half) in enumerate(((1, 1), (3, 0))):
            got = n_refs[flow].at[(c, *ring_block(flow, ring_at(flow, 4 - step), half))]
            arrived(got, *ag_sem(flow, 2 + k))
        for k, half in enumerate((0, 1)):
            got = n_refs[flow].at[(c, *ring_block(flow, ring_at(flow, 2), half))]
            arrived(got, *ag_sem(flow, 4 + k))
        pair_pieces(flow, c, (3, 4, 5))

    def up(flow, half):
        offset, width, _ = FLOWS[flow]
        core = (c, other)[half]
        if half == 1:
            pair_pieces(flow, other, range(6))
        if flow == 0:
            if half == 0:
                load_wg.wait()
                load_wu.wait()
            acc_g[half] = jnp.zeros((256, 512), F32)
            acc_u[half] = jnp.zeros((256, 512), F32)

        rows = jnp.concatenate(
            [n_refs[flow][core, k, :, :, :, :width].reshape(256, width) for k in range(4)], axis=1
        )
        for acc, weights in ((acc_g, wg_buf), (acc_u, wu_buf)):
            depth = [weights[k * QUARTER + offset : k * QUARTER + offset + width] for k in range(4)]
            acc[half] += dot(rows, jnp.concatenate(depth, axis=0))

    expert = z * 8 + y * 2 + c
    lanes = lax.broadcasted_iota(jnp.int32, (256, 128), 1)

    def activate(half):
        core = (c, other)[half]
        extra = jnp.zeros((256, 128), F32)
        for k in range(4):
            extra = extra + n_refs[LAST][core, k, :, :, :, 256:].reshape(256, 128).astype(F32)
        weight = jnp.sum(jnp.where(lanes == expert, extra, 0.0), axis=-1, keepdims=True)
        square = jnp.sum(
            jnp.where((lanes == 32) | (lanes == 33), extra, 0.0), axis=-1, keepdims=True
        )
        scale = lax.rsqrt(square * (1.0 / D) + norm_eps)
        gate = acc_g[half] * scale
        act = gate / (1.0 + jnp.exp(-gate)) * (acc_u[half] * scale)
        act_buf[half] = (act * weight).astype(BF16)

    def each(function, *arguments):
        def run(number):
            for flow in SETS[number]:
                function(*(flow if a is FLOW else a for a in arguments))

        return run

    first = (
        each(project, FLOW),
        each(ring_pass, 0, FLOW),
        each(ring_end, 0, FLOW),
        each(direct_end, 0, FLOW, 1),
        each(keep_stream, FLOW),
        each(ag_end, FLOW, 2),
        each(ag_end, FLOW, 1),
        each(ag_pass, FLOW),
        each(ag_last, FLOW),
        each(up, FLOW, 0),
        each(up, FLOW, 1),
    )
    for stage, number in FIRST_ORDER:
        first[stage](number)
    activate(1)
    activate(0)

    for copy in sends:
        copy.wait_send()
    sends.clear()

    load_wd.wait()

    def down_far(flow):
        offset, width, _ = FLOWS[flow]

        for k in range(4):
            columns = slice(k * QUARTER + offset, k * QUARTER + offset + width)
            n_refs[flow][c, k, :, :, :, :width] = (
                dot(act_buf[1], wd_buf[:, columns]).astype(BF16).reshape(4, 4, 16, width)
            )
        send(
            n_refs[flow].at[c, :, :, :, :, pl.ds(0, width)],
            far_refs[flow],
            far_send_sem.at[flow],
            far_recv_sem.at[flow],
            sibling,
        )

    def down_near(flow):
        offset, width, _ = FLOWS[flow]
        arrived(far_refs[flow], far_send_sem.at[flow], far_recv_sem.at[flow])
        for k in range(4):
            columns = slice(k * QUARTER + offset, k * QUARTER + offset + width)
            total = dot(act_buf[0], wd_buf[:, columns])
            total = total + far_refs[flow][k].reshape(256, width).astype(F32)
            p_refs[flow][k] = total.astype(BF16).reshape(4, 4, 16, width)
        ring_start(1, flow)

    def add_stream(flow):
        offset, width, _ = FLOWS[flow]
        stream_buf[:, offset : offset + width] += direct_end(1, flow, 2)

    down_far(0)
    for flow in range(6):
        if flow < 5:
            down_far(flow + 1)
        down_near(flow)
        if flow >= 3:
            ring_pass(1, flow - 3)
    for flow in range(3, 6):
        ring_pass(1, flow)
    for stage in (each(ring_end, 1, FLOW), each(direct_end, 1, FLOW, 1), each(add_stream, FLOW)):
        stage(0)
        stage(1)

    rounded = stream_buf[...].astype(BF16)
    last = jnp.zeros((64, 512), F32)
    for j in range(4):
        pick = onehot(
            (64, 16), lambda i: jnp.where((i % 16) // 4 == j, i // 16 * 4 + i % 4, -1)
        )
        piece = rounded[:, j * 512 : min(j * 512 + 512, QUARTER)]
        moved = dot(pick, piece)
        if moved.shape[1] < 512:
            moved = jnp.concatenate([moved, jnp.zeros((64, 512 - moved.shape[1]), F32)], axis=1)
        last = last + moved
    last_send[...] = last.astype(BF16).reshape(4, 16, 512)
    for step in range(1, 4):
        to = (x + step) % 4
        send(
            last_send.at[to],
            last_recv.at[x],
            last_send_sem.at[step],
            last_recv_sem.at[step],
            device(to, z, y, c),
        )
    last_recv[x] = last_send[x]
    for step in range(1, 4):
        arrived(last_recv.at[(x + 4 - step) % 4], last_send_sem.at[step], last_recv_sem.at[step])
    for k in range(4):
        quarter = last_recv[k].astype(F32)
        for j in range(4):
            width = min(512, QUARTER - j * 512)
            start = k * QUARTER + j * 512
            out_ref[0, :, start : start + width] = quarter[j * 4 : j * 4 + 4, :width].astype(BF16)
    for copy in sends:
        copy.wait_send()


def per_device(
    queries,
    compressed_cache,
    lengths,
    value_expand_matrix,
    out_proj,
    residual,
    norm_gain,
    expert_ids,
    expert_gates,
    w_gate,
    w_up,
    w_down,
):
    vmem = lambda *shape, dtype=BF16: pltpu.VMEM(shape, dtype)
    widths = [w for _, w, _ in FLOWS]
    dma = lambda *n: pltpu.SemaphoreType.DMA(n)
    scratch = [
        vmem(4, 576, 128),
        vmem(4, 576, 512),
        vmem(256, D),
        vmem(D, 512),
        vmem(D, 512),
        vmem(512, D),
        vmem(4, 512, 256),
        vmem(2, 16, 16, 512),
        vmem(2, 16, 16, 512),
        vmem(1, D, dtype=F32),
        vmem(512, 128, dtype=F32),
        vmem(4, 64, 256),
        vmem(4, 64, 256),
        tuple(vmem(4, 4, 4, 16, w) for w in widths),
        tuple(vmem(2, 2, 4, 16, w) for w in widths),
        tuple(vmem(2, 4, 4, 16, w) for w in widths),
        tuple(vmem(4, 4, 16, w) for w in widths),
        tuple(vmem(3, 4, 16, w) for w in widths),
        tuple(vmem(4, 16, w) for w in widths),
        tuple(vmem(3, 16, w) for w in widths),
        tuple(vmem(2, 4, 4, 4, 16, w + 128 * (f == LAST)) for f, w in enumerate(widths)),
        vmem(16, QUARTER, dtype=F32),
        vmem(2, 256, 512, dtype=F32),
        vmem(2, 256, 512, dtype=F32),
        vmem(2, 256, 512),
        tuple(vmem(4, 4, 4, 16, w) for w in widths),
        vmem(4, 16, 512),
        vmem(4, 16, 512),
        dma(9),
        dma(4),
        dma(4),
        dma(1),
        dma(1),
        dma(2, 16),
        dma(2, 16),
        dma(4),
        dma(4),
        dma(144),
        dma(144),
        dma(72),
        dma(72),
        dma(36),
        dma(36),
        dma(6),
        dma(6),
        dma(4),
        dma(4),
    ]
    in_vmem = pl.BlockSpec(memory_space=pltpu.VMEM)
    anywhere = pl.BlockSpec(memory_space=pl.ANY)
    result = pl.pallas_call(
        kernel,
        out_shape=jax.ShapeDtypeStruct((1, 4, D), BF16),
        in_specs=[pl.BlockSpec(memory_space=pltpu.SMEM)] + [in_vmem] * 4 + [anywhere] * 7,
        out_specs=in_vmem,
        scratch_shapes=scratch,
        compiler_params=pltpu.CompilerParams(
            collective_id=0, has_side_effects=True, vmem_limit_bytes=64 << 20
        ),
        cost_estimate=pl.CostEstimate(
            flops=14 * 10**9, bytes_accessed=28 * 10**6, transcendentals=600_000
        ),
        name="layer",
    )(
        lengths,
        residual[0],
        norm_gain,
        expert_ids[0],
        expert_gates[0],
        jnp.swapaxes(queries, 2, 3),
        jnp.swapaxes(compressed_cache, 2, 3),
        value_expand_matrix,
        out_proj,
        w_gate,
        w_up,
        w_down,
    )
    return result


def solution(mesh):
    in_specs = (
        P("grp", "role", None, None),
        P("grp", "role", None, None),
        P("grp", "role"),
        P(("role", "grp"), None, None),
        P(("role", "grp"), None),
        P("grp", "role", None),
        P(),
        P("grp", "role", None),
        P("grp", "role", None),
        P("grp", None, "role"),
        P("grp", None, "role"),
        P("grp", "role", None),
    )
    out_specs = P("grp", "role", None)
    return jax.shard_map(
        per_device, mesh=mesh, in_specs=in_specs, out_specs=out_specs, check_vma=False
    )
```

```python
import jax
import jax.numpy as jnp
from jax import lax
from jax.experimental import pallas as pl
from jax.experimental.pallas import tpu as pltpu
from jax.sharding import PartitionSpec as P

MESH = pl.DeviceIdType.MESH
F32 = jnp.float32
BF16 = jnp.bfloat16

score_scale = 192.0 ** (-0.5)
norm_eps = 1e-06

D = 7168
QUARTER = 1792
FLOWS = (
    (0, 384, (0, 1, 2)),
    (384, 256, (1, 2, 0)),
    (640, 256, (2, 0, 1)),
    (896, 256, (0, 1, 2)),
    (1152, 384, (1, 2, 0)),
    (1536, 256, (2, 0, 1)),
)
LAST = 5
SETS = ((0, 1, 2), (3, 4, 5))
FIRST_ORDER = tuple((stage, number) for stage in range(6) for number in (0, 1)) + (
    (6, 0),
    (6, 1),
    (7, 0),
    (7, 1),
    (8, 0),
    (9, 0),
    (8, 1),
    (10, 0),
    (9, 1),
    (10, 1),
)
FLOW = object()


def coordinates():
    grp = lax.axis_index("grp")
    return lax.axis_index("role"), grp // 8, (grp // 2) % 4, grp % 2


def device(x, z, y, c):
    return {"role": x, "grp": z * 8 + y * 2 + c}


def dot(a, b):
    return jnp.dot(a, b, preferred_element_type=F32)


def onehot(shape, source_of_row):
    rows = lax.broadcasted_iota(jnp.int32, shape, 0)
    columns = lax.broadcasted_iota(jnp.int32, shape, 1)
    return (columns == source_of_row(rows)).astype(BF16)


def kernel(
    len_ref,
    res_ref,
    gain_ref,
    ids_ref,
    gates_ref,
    q_hbm,
    cache_hbm,
    ve_hbm,
    op_hbm,
    wg_hbm,
    wu_hbm,
    wd_hbm,
    out_ref,
    q_buf,
    cache_buf,
    op_buf,
    wg_buf,
    wu_buf,
    wd_buf,
    ve_buf,
    a2a_send,
    a2a_recv,
    gain_f32,
    val_f32,
    val_send,
    val_recv,
    p_refs,
    x_refs,
    y_refs,
    s1_refs,
    r2_refs,
    s2_refs,
    r3_refs,
    n_refs,
    stream_buf,
    acc_g,
    acc_u,
    act_buf,
    far_refs,
    last_send,
    last_recv,
    load_sem,
    ve_send_sem,
    ve_recv_sem,
    op_send_sem,
    op_recv_sem,
    a2a_send_sem,
    a2a_recv_sem,
    val_send_sem,
    val_recv_sem,
    rs_send_sem,
    rs_recv_sem,
    ag_send_sem,
    ag_recv_sem,
    pair_send_sem,
    pair_recv_sem,
    far_send_sem,
    far_recv_sem,
    last_send_sem,
    last_recv_sem,
):
    x, z, y, c = coordinates()
    zy = z * 4 + y
    other = 1 - c
    here = (x, z, y)
    me = device(x, z, y, c)
    sibling = device(x, z, y, other)
    sends = []

    def peer(axis, step):
        at = [x, z, y]
        at[axis] = (at[axis] + step) % 4
        return device(at[0], at[1], at[2], c)

    def remote(src, dst, send_sem, recv_sem, to):
        return pltpu.make_async_remote_copy(
            src_ref=src,
            dst_ref=dst,
            send_sem=send_sem,
            recv_sem=recv_sem,
            device_id=to,
            device_id_type=MESH,
        )

    def send(src, dst, send_sem, recv_sem, to):
        copy = remote(src, dst, send_sem, recv_sem, to)
        copy.start()
        sends.append(copy)

    def arrived(dst, send_sem, recv_sem):
        remote(dst, dst, send_sem, recv_sem, me).wait_recv()

    def zy_peer(step):
        p = (zy + step) % 16
        return p, device(x, p // 4, p % 4, c)

    barrier = pltpu.get_barrier_semaphore()

    def greet(step, carry):
        _, to = zy_peer(step)
        pl.semaphore_signal(barrier, inc=1, device_id=to, device_id_type=MESH)
        return carry

    lax.fori_loop(1, 16, greet, 0)
    for step in range(1, 4):
        for core in (c, other):
            pl.semaphore_signal(
                barrier, inc=1, device_id=device((x + step) % 4, z, y, core), device_id_type=MESH
            )
    pl.semaphore_signal(barrier, inc=1, device_id=sibling, device_id_type=MESH)

    ve_own = ve_buf.at[x, :, pl.ds(pl.multiple_of(c * 128, 128), 128)]
    op_own = op_buf.at[pl.ds(pl.multiple_of(c * 128, 128), 128), :]
    load_tokens = []
    for pair in range(2):
        rows = pl.ds(2 * pair, 2)
        load_tokens.append(
            (
                pltpu.make_async_copy(q_hbm.at[0, rows], q_buf.at[rows], load_sem.at[2 * pair]),
                pltpu.make_async_copy(
                    cache_hbm.at[0, rows], cache_buf.at[rows], load_sem.at[2 * pair + 1]
                ),
            )
        )
    load_ve = pltpu.make_async_copy(ve_hbm.at[0], ve_own, load_sem.at[4])
    load_op = pltpu.make_async_copy(op_hbm, op_own, load_sem.at[5])
    load_wg = pltpu.make_async_copy(wg_hbm.at[0], wg_buf, load_sem.at[6])
    load_wu = pltpu.make_async_copy(wu_hbm.at[0], wu_buf, load_sem.at[7])
    load_wd = pltpu.make_async_copy(wd_hbm.at[0], wd_buf, load_sem.at[8])
    for load in (*load_tokens[0], *load_tokens[1], load_ve, load_op):
        load.start()

    gain_f32[...] = gain_ref[...].astype(F32).reshape(1, D)

    order = onehot((128, 128), lambda i: (i % 8) // 2 * 32 + (i // 8) * 2 + i % 2)

    def attend(t):
        query = q_buf[t]
        cache = cache_buf[t]
        scores = (
            lax.dot_general(query, cache, (((0,), (0,)), ((), ())), preferred_element_type=F32)
            * score_scale
        )
        live = lax.broadcasted_iota(jnp.int32, scores.shape, 1) < len_ref[0, t]
        top = jnp.max(jnp.where(live, scores, -1e30), axis=-1, keepdims=True)
        terms = jnp.exp(jnp.where(live, scores - top, -1e30))
        total = jnp.sum(terms, axis=-1, keepdims=True)
        latent = lax.dot_general(
            terms.astype(BF16),
            cache[:512],
            (((1,), (1,)), ((), ())),
            preferred_element_type=F32,
        )
        latent = (latent / total).astype(BF16)
        return dot(order, latent).reshape(16, 8, 512)

    def attend_pair(pair):
        for load in load_tokens[pair]:
            load.wait()
        both = jnp.concatenate([attend(2 * pair), attend(2 * pair + 1)], axis=1)
        a2a_send[pair] = both.astype(BF16)

    def a2a_start(pair):
        for step in range(1, 16):
            p, to = zy_peer(step)
            remote(
                a2a_send.at[pair, p],
                a2a_recv.at[pair, zy],
                a2a_send_sem.at[pair, step],
                a2a_recv_sem.at[pair, step],
                to,
            ).start()
        a2a_recv[pair, zy] = a2a_send[pair, zy]

    def a2a_wait(pair):
        for step in range(1, 16):
            p, to = zy_peer(16 - step)
            copy = remote(
                a2a_send.at[pair, zy],
                a2a_recv.at[pair, p],
                a2a_send_sem.at[pair, step],
                a2a_recv_sem.at[pair, step],
                to,
            )
            copy.wait_send()
            copy.wait_recv()

    attend_pair(0)
    for load in (load_wg, load_wu, load_wd):
        load.start()
    pl.semaphore_wait(barrier, 22)
    a2a_start(0)

    load_ve.wait()
    for step in range(1, 4):
        send(
            ve_own,
            ve_own,
            ve_send_sem.at[step],
            ve_recv_sem.at[step],
            device((x + step) % 4, z, y, c),
        )
    send(ve_own, ve_own, ve_send_sem.at[4], ve_recv_sem.at[4], sibling)
    load_op.wait()
    send(op_own, op_own, op_send_sem.at[0], op_recv_sem.at[0], sibling)

    attend_pair(1)
    a2a_start(1)
    for step in (1, 3, 2):
        block = ve_buf.at[(x + 4 - step) % 4, :, pl.ds(pl.multiple_of(c * 128, 128), 128)]
        arrived(block, ve_send_sem.at[step], ve_recv_sem.at[step])
        send(block, block, ve_send_sem.at[4 + step], ve_recv_sem.at[4 + step], sibling)
    a2a_wait(0)
    a2a_wait(1)
    for step in (0, 1, 3, 2):
        arrived(
            ve_buf.at[(x + 4 - step) % 4, :, pl.ds(pl.multiple_of(other * 128, 128), 128)],
            ve_send_sem.at[4 + step],
            ve_recv_sem.at[4 + step],
        )

    latents = a2a_recv[...].reshape(512, 512)
    head_of_row = lax.broadcasted_iota(jnp.int32, (512, 128), 0) % 8
    values = jnp.zeros((512, 128), F32)
    for h in range(4):
        product = dot(latents, ve_buf[h])
        values = jnp.where(head_of_row == 2 * h, product[:, :128], values)
        values = jnp.where(head_of_row == 2 * h + 1, product[:, 128:], values)
    val_f32[...] = values
    for h in range(4):
        val_send[h] = jnp.concatenate(
            [val_f32[pl.ds(2 * h, 64, stride=8), :], val_f32[pl.ds(2 * h + 1, 64, stride=8), :]],
            axis=1,
        ).astype(BF16)
    for step in range(1, 4):
        to = (x + step) % 4
        send(
            val_send.at[to],
            val_recv.at[x],
            val_send_sem.at[step],
            val_recv_sem.at[step],
            device(to, z, y, c),
        )
    val_recv[x] = val_send[x]
    arrived(
        op_buf.at[pl.ds(pl.multiple_of(other * 128, 128), 128), :],
        op_send_sem.at[0],
        op_recv_sem.at[0],
    )
    for step in range(1, 4):
        arrived(val_recv.at[(x + 4 - step) % 4], val_send_sem.at[step], val_recv_sem.at[step])

    token_order = onehot((256, 256), lambda i: (i % 16) // 4 * 64 + (i % 4) // 2 * 32 + (i // 16) * 2 + i % 2)
    rows = dot(token_order, val_recv[...].reshape(256, 256)).astype(BF16)

    own_rows = onehot((16, 4), lambda i: jnp.where(i // 4 == x, i % 4, -1))

    halves = (pl.ds(0, 2), pl.ds(2, 2))

    def ring_block(flow, index, half):
        at = [slice(None)] * 3
        first = FLOWS[flow][2][0]
        at[first] = index
        if half is not None:
            at[1 if first == 0 else 0] = halves[half]
        return tuple(at)

    def rs_sem(round_, flow, k):
        s = (round_ * 6 + flow) * 12 + k
        return rs_send_sem.at[s], rs_recv_sem.at[s]

    def ring_at(flow, step):
        return (here[FLOWS[flow][2][0]] + step) % 4

    def ring_start(round_, flow):
        axis = FLOWS[flow][2][0]
        p = p_refs[flow]
        for k, (step, block, half) in enumerate(((1, 2, 0), (3, 2, 1))):
            send(
                p.at[ring_block(flow, ring_at(flow, block), half)],
                x_refs[flow].at[k],
                *rs_sem(round_, flow, k),
                peer(axis, step),
            )
        for k, (step, half) in enumerate(((1, 1), (3, 0))):
            send(
                p.at[ring_block(flow, ring_at(flow, step), half)],
                y_refs[flow].at[k, halves[half]],
                *rs_sem(round_, flow, 2 + k),
                peer(axis, step),
            )

    def ring_pass(round_, flow):
        axis = FLOWS[flow][2][0]
        p = p_refs[flow]
        for k, (step, half) in enumerate(((1, 0), (3, 1))):
            arrived(x_refs[flow].at[k], *rs_sem(round_, flow, k))
            own = p.at[ring_block(flow, ring_at(flow, step), half)]
            own[...] = (own[...].astype(F32) + x_refs[flow][k].astype(F32)).astype(BF16)
            send(
                own,
                y_refs[flow].at[k, halves[half]],
                *rs_sem(round_, flow, 4 + k),
                peer(axis, step),
            )

    def ring_end(round_, flow):
        for k, half in ((0, 1), (1, 0)):
            arrived(y_refs[flow].at[k, halves[half]], *rs_sem(round_, flow, 2 + k))
        for k, half in ((0, 0), (1, 1)):
            arrived(y_refs[flow].at[k, halves[half]], *rs_sem(round_, flow, 4 + k))
        own = p_refs[flow].at[ring_block(flow, ring_at(flow, 0), None)]
        y_ref = y_refs[flow]
        total = own[...].astype(F32) + y_ref[0].astype(F32) + y_ref[1].astype(F32)
        s1_refs[flow][...] = total.astype(BF16)
        direct_start(round_, flow, 1)

    def direct_block(flow, phase, index):
        if phase == 2:
            return s2_refs[flow].at[index]
        _, axis, last = FLOWS[flow][2]
        return s1_refs[flow].at[(index,) if axis < last else (slice(None), index)]

    def direct_start(round_, flow, phase):
        axis = FLOWS[flow][2][phase]
        received = (r2_refs if phase == 1 else r3_refs)[flow]
        for step in range(1, 4):
            send(
                direct_block(flow, phase, (here[axis] + step) % 4),
                received.at[step - 1],
                *rs_sem(round_, flow, 3 + 3 * phase + step - 1),
                peer(axis, step),
            )

    def direct_end(round_, flow, phase):
        axis = FLOWS[flow][2][phase]
        received = (r2_refs if phase == 1 else r3_refs)[flow]
        for step in range(1, 4):
            arrived(received.at[step - 1], *rs_sem(round_, flow, 3 + 3 * phase + step - 1))
        total = direct_block(flow, phase, here[axis])[...].astype(F32)
        for k in range(3):
            total = total + received[k].astype(F32)
        if phase == 2:
            return total
        s2_refs[flow][...] = total.astype(BF16)
        direct_start(round_, flow, 2)
        return None

    def project(flow):
        offset, width, _ = FLOWS[flow]

        for k in range(4):
            columns = slice(k * QUARTER + offset, k * QUARTER + offset + width)
            p_refs[flow][k] = dot(rows, op_buf[:, columns]).astype(BF16).reshape(4, 4, 16, width)
            own = p_refs[flow].at[k, z, y]
            own[...] = (own[...].astype(F32) + dot(own_rows, res_ref[:, columns])).astype(BF16)
        ring_start(0, flow)

    squares = []

    def keep_stream(flow):
        offset, width, _ = FLOWS[flow]
        result = direct_end(0, flow, 2)
        stream_buf[:, offset : offset + width] = result
        squares.append(jnp.sum(result * result, axis=-1, keepdims=True))
        columns = pl.ds(pl.multiple_of(x * QUARTER + offset, 128), width)
        n_refs[flow][c, x, z, y, :, :width] = (result * gain_f32[:, columns]).astype(BF16)
        if flow == LAST:
            lane = lax.broadcasted_iota(jnp.int32, (4, 128), 1)
            table = jnp.zeros((4, 128), F32)
            gates = gates_ref[...].astype(F32)
            for k in range(8):
                table = table + jnp.where(ids_ref[:, k : k + 1] == lane, gates[:, k : k + 1], 0.0)
            table = dot(own_rows, table.astype(BF16))
            square = sum(squares)
            high = square.astype(BF16).astype(F32)
            lane16 = lax.broadcasted_iota(jnp.int32, (16, 128), 1)
            extra = jnp.where(lane16 == 32, high, jnp.where(lane16 == 33, square - high, table))
            n_refs[flow][c, x, z, y, :, width:] = extra.astype(BF16)
        ag_start(flow, 2)

    def ag_sem(flow, k):
        s = flow * 12 + k
        return ag_send_sem.at[s], ag_recv_sem.at[s]

    def ag_block(flow, phase, index):
        axes = FLOWS[flow][2]
        at = [slice(None)] * 3
        for a in axes[:phase]:
            at[a] = here[a]
        at[axes[phase]] = index
        return n_refs[flow].at[(c, *at)]

    def ag_start(flow, phase):
        axis = FLOWS[flow][2][phase]
        own = ag_block(flow, phase, here[axis])
        for step in range(1, 4):
            send(own, own, *ag_sem(flow, 3 + 3 * phase + step - 1), peer(axis, step))

    def ag_end(flow, phase):
        axis = FLOWS[flow][2][phase]
        for step in range(1, 4):
            arrived(
                ag_block(flow, phase, (here[axis] + 4 - step) % 4),
                *ag_sem(flow, 3 + 3 * phase + step - 1),
            )
        if phase == 2:
            ag_start(flow, 1)
        else:
            for k, (step, half) in enumerate(((1, 0), (3, 1), (1, 1), (3, 0))):
                own = n_refs[flow].at[(c, *ring_block(flow, ring_at(flow, 0), half))]
                send(own, own, *ag_sem(flow, k), peer(FLOWS[flow][2][0], step))
            pair_pieces(flow, c, (0,))

    def pair_piece(flow, core, k, index, half):
        piece = n_refs[flow].at[(core, *ring_block(flow, index, half))]
        s = flow * 6 + k
        if core is c:
            send(piece, piece, pair_send_sem.at[s], pair_recv_sem.at[s], sibling)
        else:
            arrived(piece, pair_send_sem.at[s], pair_recv_sem.at[s])

    pieces = ((0, None), (3, 0), (1, 1), (3, 1), (1, 0), (2, None))

    def pair_pieces(flow, core, numbers):
        for k in numbers:
            step, half = pieces[k]
            pair_piece(flow, core, k, ring_at(flow, step), half)

    def ag_pass(flow):
        for k, (step, half) in enumerate(((1, 0), (3, 1))):
            got = n_refs[flow].at[(c, *ring_block(flow, ring_at(flow, 4 - step), half))]
            arrived(got, *ag_sem(flow, k))
            send(got, got, *ag_sem(flow, 4 + k), peer(FLOWS[flow][2][0], step))
        pair_pieces(flow, c, (1, 2))

    def ag_last(flow):
        for k, (step, half) in enumerate(((1, 1), (3, 0))):
            got = n_refs[flow].at[(c, *ring_block(flow, ring_at(flow, 4 - step), half))]
            arrived(got, *ag_sem(flow, 2 + k))
        for k, half in enumerate((0, 1)):
            got = n_refs[flow].at[(c, *ring_block(flow, ring_at(flow, 2), half))]
            arrived(got, *ag_sem(flow, 4 + k))
        pair_pieces(flow, c, (3, 4, 5))

    def up(flow, half):
        offset, width, _ = FLOWS[flow]
        core = (c, other)[half]
        if half == 1:
            pair_pieces(flow, other, range(6))
        if flow == 0:
            if half == 0:
                load_wg.wait()
                load_wu.wait()
            acc_g[half] = jnp.zeros((256, 512), F32)
            acc_u[half] = jnp.zeros((256, 512), F32)

        rows = jnp.concatenate(
            [n_refs[flow][core, k, :, :, :, :width].reshape(256, width) for k in range(4)], axis=1
        )
        for acc, weights in ((acc_g, wg_buf), (acc_u, wu_buf)):
            depth = [weights[k * QUARTER + offset : k * QUARTER + offset + width] for k in range(4)]
            acc[half] += dot(rows, jnp.concatenate(depth, axis=0))

    expert = z * 8 + y * 2 + c
    lanes = lax.broadcasted_iota(jnp.int32, (256, 128), 1)

    def activate(half):
        core = (c, other)[half]
        extra = jnp.zeros((256, 128), F32)
        for k in range(4):
            extra = extra + n_refs[LAST][core, k, :, :, :, FLOWS[LAST][1] :].reshape(256, 128).astype(F32)
        weight = jnp.sum(jnp.where(lanes == expert, extra, 0.0), axis=-1, keepdims=True)
        square = jnp.sum(
            jnp.where((lanes == 32) | (lanes == 33), extra, 0.0), axis=-1, keepdims=True
        )
        scale = lax.rsqrt(square * (1.0 / D) + norm_eps)
        gate = acc_g[half] * scale
        act = gate / (1.0 + jnp.exp(-gate)) * (acc_u[half] * scale)
        act_buf[half] = (act * weight).astype(BF16)

    def each(function, *arguments):
        def run(number):
            for flow in SETS[number]:
                function(*(flow if a is FLOW else a for a in arguments))

        return run

    first = (
        each(project, FLOW),
        each(ring_pass, 0, FLOW),
        each(ring_end, 0, FLOW),
        each(direct_end, 0, FLOW, 1),
        each(keep_stream, FLOW),
        each(ag_end, FLOW, 2),
        each(ag_end, FLOW, 1),
        each(ag_pass, FLOW),
        each(ag_last, FLOW),
        each(up, FLOW, 0),
        each(up, FLOW, 1),
    )
    for stage, number in FIRST_ORDER:
        first[stage](number)
    activate(1)
    activate(0)

    for copy in sends:
        copy.wait_send()
    sends.clear()

    load_wd.wait()

    def down_far(flow):
        offset, width, _ = FLOWS[flow]

        for k in range(4):
            columns = slice(k * QUARTER + offset, k * QUARTER + offset + width)
            n_refs[flow][c, k, :, :, :, :width] = (
                dot(act_buf[1], wd_buf[:, columns]).astype(BF16).reshape(4, 4, 16, width)
            )
        send(
            n_refs[flow].at[c, :, :, :, :, pl.ds(0, width)],
            far_refs[flow],
            far_send_sem.at[flow],
            far_recv_sem.at[flow],
            sibling,
        )

    def down_near(flow):
        offset, width, _ = FLOWS[flow]
        arrived(far_refs[flow], far_send_sem.at[flow], far_recv_sem.at[flow])
        for k in range(4):
            columns = slice(k * QUARTER + offset, k * QUARTER + offset + width)
            total = dot(act_buf[0], wd_buf[:, columns])
            total = total + far_refs[flow][k].reshape(256, width).astype(F32)
            p_refs[flow][k] = total.astype(BF16).reshape(4, 4, 16, width)
        ring_start(1, flow)

    def add_stream(flow):
        offset, width, _ = FLOWS[flow]
        stream_buf[:, offset : offset + width] += direct_end(1, flow, 2)

    count = len(FLOWS)
    down_far(0)
    for flow in range(count):
        if flow < count - 1:
            down_far(flow + 1)
        down_near(flow)
    for flow in range(count):
        ring_pass(1, flow)
    for stage in (each(ring_end, 1, FLOW), each(direct_end, 1, FLOW, 1), each(add_stream, FLOW)):
        stage(0)
        stage(1)

    rounded = stream_buf[...].astype(BF16)
    last = jnp.zeros((64, 512), F32)
    for j in range(4):
        pick = onehot(
            (64, 16), lambda i: jnp.where((i % 16) // 4 == j, i // 16 * 4 + i % 4, -1)
        )
        piece = rounded[:, j * 512 : min(j * 512 + 512, QUARTER)]
        moved = dot(pick, piece)
        if moved.shape[1] < 512:
            moved = jnp.concatenate([moved, jnp.zeros((64, 512 - moved.shape[1]), F32)], axis=1)
        last = last + moved
    last_send[...] = last.astype(BF16).reshape(4, 16, 512)
    for step in range(1, 4):
        to = (x + step) % 4
        send(
            last_send.at[to],
            last_recv.at[x],
            last_send_sem.at[step],
            last_recv_sem.at[step],
            device(to, z, y, c),
        )
    last_recv[x] = last_send[x]
    for step in range(1, 4):
        arrived(last_recv.at[(x + 4 - step) % 4], last_send_sem.at[step], last_recv_sem.at[step])
    for k in range(4):
        quarter = last_recv[k].astype(F32)
        for j in range(4):
            width = min(512, QUARTER - j * 512)
            start = k * QUARTER + j * 512
            out_ref[0, :, start : start + width] = quarter[j * 4 : j * 4 + 4, :width].astype(BF16)
    for copy in sends:
        copy.wait_send()


def per_device(
    queries,
    compressed_cache,
    lengths,
    value_expand_matrix,
    out_proj,
    residual,
    norm_gain,
    expert_ids,
    expert_gates,
    w_gate,
    w_up,
    w_down,
):
    vmem = lambda *shape, dtype=BF16: pltpu.VMEM(shape, dtype)
    widths = [w for _, w, _ in FLOWS]
    dma = lambda *n: pltpu.SemaphoreType.DMA(n)
    scratch = [
        vmem(4, 576, 128),
        vmem(4, 576, 512),
        vmem(256, D),
        vmem(D, 512),
        vmem(D, 512),
        vmem(512, D),
        vmem(4, 512, 256),
        vmem(2, 16, 16, 512),
        vmem(2, 16, 16, 512),
        vmem(1, D, dtype=F32),
        vmem(512, 128, dtype=F32),
        vmem(4, 64, 256),
        vmem(4, 64, 256),
        tuple(vmem(4, 4, 4, 16, w) for w in widths),
        tuple(vmem(2, 2, 4, 16, w) for w in widths),
        tuple(vmem(2, 4, 4, 16, w) for w in widths),
        tuple(vmem(4, 4, 16, w) for w in widths),
        tuple(vmem(3, 4, 16, w) for w in widths),
        tuple(vmem(4, 16, w) for w in widths),
        tuple(vmem(3, 16, w) for w in widths),
        tuple(vmem(2, 4, 4, 4, 16, w + 128 * (f == LAST)) for f, w in enumerate(widths)),
        vmem(16, QUARTER, dtype=F32),
        vmem(2, 256, 512, dtype=F32),
        vmem(2, 256, 512, dtype=F32),
        vmem(2, 256, 512),
        tuple(vmem(4, 4, 4, 16, w) for w in widths),
        vmem(4, 16, 512),
        vmem(4, 16, 512),
        dma(9),
        dma(8),
        dma(8),
        dma(1),
        dma(1),
        dma(2, 16),
        dma(2, 16),
        dma(4),
        dma(4),
        dma(144),
        dma(144),
        dma(72),
        dma(72),
        dma(36),
        dma(36),
        dma(6),
        dma(6),
        dma(4),
        dma(4),
    ]
    in_vmem = pl.BlockSpec(memory_space=pltpu.VMEM)
    anywhere = pl.BlockSpec(memory_space=pl.ANY)
    result = pl.pallas_call(
        kernel,
        out_shape=jax.ShapeDtypeStruct((1, 4, D), BF16),
        in_specs=[pl.BlockSpec(memory_space=pltpu.SMEM)] + [in_vmem] * 4 + [anywhere] * 7,
        out_specs=in_vmem,
        scratch_shapes=scratch,
        compiler_params=pltpu.CompilerParams(
            collective_id=0, has_side_effects=True, vmem_limit_bytes=64 << 20
        ),
        cost_estimate=pl.CostEstimate(
            flops=14 * 10**9, bytes_accessed=28 * 10**6, transcendentals=600_000
        ),
        name="layer",
    )(
        lengths,
        residual[0],
        norm_gain,
        expert_ids[0],
        expert_gates[0],
        jnp.swapaxes(queries, 2, 3),
        jnp.swapaxes(compressed_cache, 2, 3),
        value_expand_matrix,
        out_proj,
        w_gate,
        w_up,
        w_down,
    )
    return result


def solution(mesh):
    in_specs = (
        P("grp", "role", None, None),
        P("grp", "role", None, None),
        P("grp", "role"),
        P(("role", "grp"), None, None),
        P(("role", "grp"), None),
        P("grp", "role", None),
        P(),
        P("grp", "role", None),
        P("grp", "role", None),
        P("grp", None, "role"),
        P("grp", None, "role"),
        P("grp", "role", None),
    )
    out_specs = P("grp", "role", None)
    return jax.shard_map(
        per_device, mesh=mesh, in_specs=in_specs, out_specs=out_specs, check_vma=False
    )
```
